256 devices in a mesh: vol: 16 (over x, y), sp: 16 (over z, core).
Axes of the slice: x: 4, y: 4, z: 8, core: 2. Of those that a mesh axis runs over, the one named last changes fastest.
Arguments:
- volume: bfloat16 [16, 16, 32, 32, 128], P('vol', 'sp'), may hold values from -6 to 6
- conv_weight: bfloat16 [3, 3, 3, 128, 256], replicated, may hold values from -0.109375 to 0.109375
- group_weight: bfloat16 [3, 3, 8, 256], replicated, may hold values from -0.75 to 0.75
- slice_count: int32 [16], P('vol'), may hold values from 5 to 16
- pooled_grad: float32 [16, 256], P('vol'), may hold values from -48 to 48
Outputs:
- grad_conv: float32 [3, 3, 3, 128, 256], P(None, None, None, None, 'sp')
- grad_group: float32 [3, 3, 8, 256], P(None, None, None, 'sp')
The draws below stay inside these ranges and needn't reach their ends.
All inputs are finite; a program needn't handle non-finite values.
Results may differ from the reference program's by a relative error of at most 0.028.
The reference program's roundings to bfloat16 on the way (of `hidden`, `d_summed` and `d_pre`) count: a program that leaves them out, or rounds other values in their place, can miss the bound.
Values may be sent and summed in bfloat16 or wider, within the bound.
A program may use at most 128 MiB of HBM per device.

```python
import jax
import jax.numpy as jnp
from jax import lax

H = 32
C_IN = 128
C_OUT = 256
GROUP = 8
VOLS = 16
DEPTH = 16


def set_ends(result, own_key, low, top_value):
    spot = [jax.random.randint(jax.random.fold_in(own_key, axis), (), 0, length) for axis, length in enumerate(result.shape)]
    longest = result.shape.index(max(result.shape))
    neighbour = spot[:longest] + [(spot[longest] + 1) % result.shape[longest]] + spot[longest + 1:]
    return result.at[tuple(spot)].set(low).at[tuple(neighbour)].set(top_value)


def steps_of(key, extent, cuts, low, high):
    loudness = 1.0
    for axis_at, shards_of in cuts:
        draws = jax.random.uniform(jax.random.fold_in(jax.random.fold_in(key, 6), axis_at), (shards_of,), jnp.float32, low / len(cuts), high / len(cuts))
        loudness = loudness * jnp.repeat(jnp.exp(draws), extent[axis_at] // shards_of).reshape((-1,) + (1,) * (len(extent) - 1 - axis_at))
    return loudness


def noise(key, dims, deviation, reach, shards=(), dtype=jnp.bfloat16):
    entries = jax.random.normal(key, dims, jnp.float32) * deviation
    if len(shards) > 0:
        entries = steps_of(key, dims, shards, -0.22, 0.18) * entries
    return jnp.clip(entries, min=-reach, max=reach).astype(dtype)


def setup_inputs(seed: int = 0) -> dict:
    arg_keys = jax.random.split(jax.random.key(seed), 6)
    return {
        "volume": noise(arg_keys[0], (VOLS, DEPTH, H, H, C_IN), 1.0, 6.0, ((0, 16), (1, 16))),
        "conv_weight": noise(arg_keys[1], (3, 3, 3, C_IN, C_OUT), (27 * C_IN) ** -0.5, 0.109375),
        "group_weight": noise(arg_keys[2], (3, 3, GROUP, C_OUT), (9 * GROUP) ** -0.5, 0.75),
        "slice_count": set_ends(jax.random.randint(arg_keys[3], (VOLS,), DEPTH // 3, DEPTH + 1), jax.random.fold_in(arg_keys[3], 1), DEPTH // 3, DEPTH).astype(jnp.int32),
        "pooled_grad": noise(arg_keys[4], (VOLS, C_OUT), 8.0, 48.0, ((0, 16),), jnp.float32),
    }


LAYOUT = ('NDHWC', 'DHWIO', 'NDHWC')

def convolve(padded, kernel, strides, group_count):
    return lax.conv_general_dilated(padded, kernel, strides, 'VALID', dimension_numbers=LAYOUT, feature_group_count=group_count, preferred_element_type=jnp.float32)

def conv_grad(padded, upstream, depth_len, row_count, col_count):
    inputs = padded.shape[-1]
    flat_up = upstream.reshape(-1, upstream.shape[-1])
    pieces = []
    for slab_tap in range(3):
        for row_tap in range(3):
            for col_tap in range(3):
                window = padded[:, slab_tap:slab_tap + depth_len, row_tap:row_tap + 2 * row_count - 1:2, col_tap:col_tap + 2 * col_count - 1:2, :]
                pieces.append(jnp.dot(window.reshape(-1, inputs).T, flat_up, preferred_element_type=jnp.float32))
    return jnp.stack(pieces).reshape(3, 3, 3, inputs, flat_up.shape[-1])

def group_terms(hpad, dpad, dsum, group_weight, row_count, col_count):
    group_size = group_weight.shape[2]
    channels = group_weight.shape[3]
    group_count = channels // group_size
    flat_d = dsum.reshape(-1, group_count, group_size).astype(jnp.float32)
    backward = flat_d
    pieces = []
    for row_tap in range(3):
        for col_tap in range(3):
            window = hpad[:, :, row_tap:row_tap + row_count, col_tap:col_tap + col_count, :].reshape(-1, group_count, group_size)
            pieces.append(jnp.einsum('pqk,pqo->kqo', window.astype(jnp.float32), flat_d).reshape(group_size, channels))
            shifted = dpad[:, :, 2 - row_tap:2 - row_tap + row_count, 2 - col_tap:2 - col_tap + col_count, :].reshape(-1, group_count, group_size)
            kernel = group_weight[row_tap, col_tap].reshape(group_size, group_count, group_size)
            backward = backward + jnp.einsum('pqo,kqo->pqk', shifted.astype(jnp.float32), kernel.astype(jnp.float32))
    return (jnp.stack(pieces).reshape(3, 3, group_size, channels), backward.reshape(dsum.shape))

def one_volume(volume_one, count, grad_row, conv_weight, group_weight):
    depth_len = volume_one.shape[0]
    half_width = volume_one.shape[1] // 2
    group_count = group_weight.shape[3] // group_weight.shape[2]
    padded = jnp.pad(volume_one[None], ((0, 0), (1, 1), (1, 1), (1, 1), (0, 0)))
    pre = convolve(padded, conv_weight, (1, 2, 2), 1)
    alive = (jnp.arange(depth_len) < count).astype(jnp.float32)[None, :, None, None, None]
    hidden = (jnp.maximum(pre, 0.0) * alive).astype(jnp.bfloat16)
    hpad = jnp.pad(hidden, ((0, 0), (0, 0), (1, 1), (1, 1), (0, 0)))
    mixed = convolve(hpad, group_weight[None], (1, 1, 1), group_count)
    summed = hidden.astype(jnp.float32) + mixed
    scale = 1.0 / (count.astype(jnp.float32) * half_width * half_width)
    d_summed = jnp.where(summed > 0, grad_row[None, None, None, None, :] * alive * scale, 0.0).astype(jnp.bfloat16)
    dpad = jnp.pad(d_summed, ((0, 0), (0, 0), (1, 1), (1, 1), (0, 0)))
    grad_group, d_hidden = group_terms(hpad, dpad, d_summed, group_weight, half_width, half_width)
    d_pre = (jnp.where(pre > 0, d_hidden, 0.0) * alive).astype(jnp.bfloat16)
    grad_conv = conv_grad(padded, d_pre, depth_len, half_width, half_width)
    return (grad_conv, grad_group)

def reference(volume, conv_weight, group_weight, slice_count, pooled_grad):

    def per_volume(items):
        return one_volume(items[0], items[1], items[2], conv_weight, group_weight)
    conv_all, group_all = lax.map(per_volume, (volume, slice_count, pooled_grad))
    return (lax.optimization_barrier(jnp.sum(conv_all, axis=0)), lax.optimization_barrier(jnp.sum(group_all, axis=0)))
```

```python
import jax
import jax.numpy as jnp
from jax import lax
from jax.experimental import pallas as pl
from jax.experimental.pallas import tpu as pltpu
from jax.sharding import PartitionSpec as P

BF16 = jnp.bfloat16
F32 = jnp.float32
REDUCERS = 15


def remote(src, dst, send, recv, device):
    return pltpu.make_async_remote_copy(
        src_ref=src,
        dst_ref=dst,
        send_sem=send,
        recv_sem=recv,
        device_id=device,
        device_id_type=pl.DeviceIdType.MESH,
    )


def dot(left, right):
    return jnp.dot(left, right, preferred_element_type=F32)


def dot_nt(left, right):
    return lax.dot_general(left, right, (((1,), (1,)), ((), ())), preferred_element_type=F32)


def one_where(condition):
    return jnp.where(condition, 1.0, 0.0).astype(BF16)


def iota(shape, dim):
    return lax.broadcasted_iota(jnp.int32, shape, dim)


def kernel(
    vol,
    w,
    gw,
    cnt,
    pg,
    conv_out,
    group_out,
    volb,
    wv,
    xs,
    pick,
    shift,
    wg,
    hk,
    dk,
    dts,
    ggs,
    dx,
    gx,
    part,
    r1,
    s2,
    r2,
    f3,
    outb,
    loc_sem,
    halo_send,
    halo_recv,
    dx_send,
    dx_recv,
    s1_send,
    s1_recv,
    s2_send,
    s2_recv,
    s3_send,
    s3_recv,
):
    v = lax.axis_index("vol")
    sp = lax.axis_index("sp")
    x, y = lax.div(v, 4), lax.rem(v, 4)
    z, core = lax.div(sp, 2), lax.rem(sp, 2)
    sib = (v, z * 2 + 1 - core)
    far = (v, lax.rem(sp + 15 + 2 * core, 16))

    def vol_peer(i):
        return lax.rem(x + lax.div(i, 4), 4) * 4 + lax.rem(y + lax.rem(i, 4), 4)

    def z_peer(i):
        return lax.rem(z + i, 8)

    own_copy = pltpu.make_async_copy(vol, volb.at[1 + core], loc_sem.at[0])
    own_copy.start()
    w_copy = pltpu.make_async_copy(w, wv, loc_sem.at[1])
    w_copy.start()

    barrier = pltpu.get_barrier_semaphore()

    def greet(device):
        pl.semaphore_signal(barrier, inc=1, device_id=device, device_id_type=pl.DeviceIdType.MESH)

    greet(sib)
    greet(far)

    def greet_vol(i, carry):
        greet((vol_peer(i), sp))
        return carry

    def greet_z(i, carry):
        greet((v, z_peer(i) * 2 + core))
        return carry

    lax.fori_loop(1, 16, greet_vol, 0)
    lax.fori_loop(1, 8, greet_z, 0)

    m = iota((384, 256), 0)
    tap, within = lax.div(m, 128), lax.rem(m, 128)
    row = 2 * lax.div(lax.rem(within, 64), 16) + lax.div(within, 64)
    col = 2 * lax.rem(within, 16) + tap - 1
    pick[...] = one_where((iota((384, 256), 1) == row * 32 + col) & (col >= 0))

    pl.semaphore_wait(barrier, 24)
    to_sib = remote(vol, volb.at[1 + core], halo_send.at[0], halo_recv.at[0], sib)
    to_far = remote(vol, volb.at[3 - 3 * core], halo_send.at[1], halo_recv.at[1], far)
    to_far.start()
    to_sib.start()

    m, n = iota((256, 256), 0), iota((256, 256), 1)
    in_row = lax.rem(m, 16)
    shift[0] = one_where((n == m - 1) & (in_row != 0))
    shift[1] = one_where((n == m + 1) & (in_row != 15))
    same_group = lax.div(m, 8) == lax.div(n, 8)
    for jk in range(9):
        tiled = jnp.broadcast_to(gw[jk].astype(F32)[None], (32, 8, 256)).reshape(256, 256)
        wg[jk] = jnp.where(same_group, tiled, 0.0).astype(BF16)
    for k in range(3):
        hk[k, 0:16, :] = jnp.zeros((16, 256), BF16)
        hk[k, 272:288, :] = jnp.zeros((16, 256), BF16)
        dk[k, 0:16, :] = jnp.zeros((16, 256), BF16)
        dk[k, 272:288, :] = jnp.zeros((16, 256), BF16)

    def windows(slot, inside):
        xs[slot, 0:16, 0:384] = jnp.zeros((16, 384), BF16)
        xs[slot, :, 1152:1280] = jnp.zeros((272, 128), BF16)
        for block in range(4):
            picked = dot(pick[...], volb[slot, 256 * block : 256 * block + 256, :])
            if inside is not None:
                picked = picked * inside
            picked = picked.astype(BF16)
            for e in range(3):
                even = picked[e * 128 : e * 128 + 64]
                odd = picked[e * 128 + 64 : e * 128 + 128]
                for b, rows, offset in ((0, odd, 16), (1, even, 0), (2, odd, 0)):
                    lane = (b * 3 + e) * 128
                    start = 64 * block + offset
                    xs[slot, start : start + 64, lane : lane + 128] = rows

    at_low = jnp.where(z == 0, 0.0, 1.0)
    at_high = jnp.where(z == 7, 0.0, 1.0)
    far_inside = jnp.where(core == 0, at_low, at_high)
    beyond_inside = jnp.where(core == 0, at_high, at_low)

    own_copy.wait()
    windows(1 + core, None)
    remote(vol, volb.at[2 - core], halo_send.at[0], halo_recv.at[0], sib).wait_recv()
    windows(2 - core, None)
    remote(vol, volb.at[3 * core], halo_send.at[1], halo_recv.at[1], far).wait_recv()
    relay = remote(
        volb.at[3 * core], volb.at[3 * core], halo_send.at[2], halo_recv.at[2], sib
    )
    relay.start()
    windows(3 * core, far_inside)
    w_copy.wait()

    pre = dot(xs[core, 0:256, 0:1152], wv[0])
    pre = pre + dot(xs[core + 1, 0:256, 0:1152], wv[1])
    pre = pre + dot(xs[core + 2, 0:256, 0:1152], wv[2])

    count = cnt[0]
    live = jnp.where(sp < count, 1.0, 0.0)
    hidden = (jnp.maximum(pre, 0.0) * live).astype(BF16)
    hk[1, 16:272, :] = hidden
    hk[0, 16:272, :] = dot(shift[0], hidden).astype(BF16)
    hk[2, 16:272, :] = dot(shift[1], hidden).astype(BF16)
    summed = hidden.astype(F32)
    for j in range(3):
        for k in range(3):
            summed = summed + dot(hk[k, 16 * j : 16 * j + 256, :], wg[3 * j + k])
    scale = 1.0 / jnp.full((1, 256), count.astype(F32) * 256.0)
    cotangent = pg[...] * live * scale
    d_wide = jnp.where(summed > 0, cotangent, 0.0)
    d_summed = d_wide.astype(BF16)
    dk[1, 16:272, :] = d_summed
    dk[0, 16:272, :] = dot(shift[0], d_summed).astype(BF16)
    dk[2, 16:272, :] = dot(shift[1], d_summed).astype(BF16)
    d_hidden = d_summed.astype(F32)
    for j in range(3):
        for k in range(3):
            lines = dk[2 - k, 16 * (2 - j) : 16 * (2 - j) + 256, :]
            d_hidden = d_hidden + dot_nt(lines, wg[3 * j + k])
    d_pre = jnp.where(pre > 0, d_hidden, 0.0) * live
    turned = d_pre.T.astype(BF16)
    for t in range(8):
        for c in range(2):
            start = 16 * (2 * t + c)
            dts[c, 16 * t : 16 * t + 16, :] = turned[start : start + 16, :]
    swap_d = remote(dts.at[1 - core], dx, dx_send.at[0], dx_recv.at[0], sib)
    swap_d.start()

    d_turned = d_wide.T.astype(BF16)
    fold = one_where(lax.rem(iota((256, 128), 0), 8) == lax.rem(iota((256, 128), 1), 8))
    lane_tap = lax.div(iota((256, 128), 1), 8)
    grouped = jnp.zeros((256, 128), F32)
    for j in range(3):
        for k in range(3):
            full = dot(d_turned, hk[k, 16 * j : 16 * j + 256, :])
            kept = jnp.where(same_group, full, 0.0).astype(BF16)
            grouped = jnp.where(lane_tap == 3 * j + k, dot(kept, fold), grouped)
    grouped = grouped.astype(BF16)
    for t in range(8):
        for c in range(2):
            start = 16 * (2 * t + c)
            ggs[c, 16 * t : 16 * t + 16, :] = grouped[start : start + 16, :]
    swap_g = remote(ggs.at[1 - core], gx, dx_send.at[1], dx_recv.at[1], sib)
    swap_g.start()

    remote(
        volb.at[3 - 3 * core], volb.at[3 - 3 * core], halo_send.at[2], halo_recv.at[2], sib
    ).wait_recv()
    windows(3 - 3 * core, beyond_inside)
    swap_d.wait_recv()
    swap_g.wait_recv()

    def partial(i, carry):
        to = vol_peer(i)

        @pl.when(to < REDUCERS)
        def _():
            a = lax.div(to, 5)
            lanes = pl.ds(pl.multiple_of(lax.rem(to, 5) * 256, 256), 256)
            total = dot(dts[core], xs[core + a, 0:256, lanes])
            total = total + dot(dx[...], xs[1 - core + a, 0:256, lanes])
            low = total[:, 0:128].astype(BF16)
            extra = (ggs[core].astype(F32) + gx[...].astype(F32)) * jnp.where(
                to == REDUCERS - 1, 1.0, 0.0
            )
            high = (total[:, 128:256] + extra).astype(BF16)

            @pl.when(i == 0)
            def _():
                r1[v, 0] = low
                r1[v, 1] = high

            @pl.when(i > 0)
            def _():
                part[to, 0] = low
                part[to, 1] = high
                remote(
                    part.at[to], r1.at[v], s1_send.at[to], s1_recv.at[v], (to, sp)
                ).start()

        return carry

    lax.fori_loop(0, 16, partial, 0)

    @pl.when(v < REDUCERS)
    def _():
        def add(i, carry):
            source = vol_peer(i)
            remote(
                part.at[0], r1.at[source], s1_send.at[0], s1_recv.at[source], (source, sp)
            ).wait_recv()
            return tuple(carry[h] + r1[source, h].astype(F32) for h in range(2))

        start = tuple(r1[v, h].astype(F32) for h in range(2))
        sums = lax.fori_loop(1, 16, add, start)
        for t in range(8):
            for h in range(2):
                s2[t, h] = sums[h][16 * t : 16 * t + 16, :]

        def send_z(i, carry):
            to = z_peer(i)
            remote(
                s2.at[to], r2.at[z], s2_send.at[to], s2_recv.at[z], (v, to * 2 + core)
            ).start()
            return carry

        lax.fori_loop(1, 8, send_z, 0)

        def add_z(i, carry):
            source = z_peer(i)
            remote(
                s2.at[0], r2.at[source], s2_send.at[0], s2_recv.at[source], (v, source * 2 + core)
            ).wait_recv()
            return carry + r2[source]

        final = lax.fori_loop(1, 8, add_z, s2[z])
        f3[...] = final
        outb[v] = final

        def spread(i, carry):
            to = vol_peer(i)
            remote(f3, outb.at[v], s3_send.at[to], s3_recv.at[v], (to, sp)).start()
            return carry

        lax.fori_loop(1, 16, spread, 0)

    def collect(i, carry):
        source = vol_peer(i)

        @pl.when(source < REDUCERS)
        def _():
            remote(
                f3, outb.at[source], s3_send.at[0], s3_recv.at[source], (source, sp)
            ).wait_recv()

        return carry

    lax.fori_loop(1, 16, collect, 0)
    for a in range(3):
        for t in range(9):
            conv_out[9 * a + t] = outb[5 * a + t // 2, t % 2]
    last = jnp.concatenate([outb[REDUCERS - 1, 1], jnp.zeros((112, 128), F32)], axis=0)
    group_out[...] = last.T[0:72, 0:16]

    to_sib.wait_send()
    to_far.wait_send()
    relay.wait_send()
    swap_d.wait_send()
    swap_g.wait_send()

    def drain_vol(i, carry):
        to = vol_peer(i)

        @pl.when(to < REDUCERS)
        def _():
            remote(part.at[to], r1.at[v], s1_send.at[to], s1_recv.at[v], (to, sp)).wait_send()

        @pl.when(v < REDUCERS)
        def _():
            remote(f3, outb.at[v], s3_send.at[to], s3_recv.at[v], (to, sp)).wait_send()

        return carry

    lax.fori_loop(1, 16, drain_vol, 0)

    @pl.when(v < REDUCERS)
    def _():
        def drain_z(i, carry):
            to = z_peer(i)
            remote(
                s2.at[to], r2.at[z], s2_send.at[to], s2_recv.at[z], (v, to * 2 + core)
            ).wait_send()
            return carry

        lax.fori_loop(1, 8, drain_z, 0)


def local(volume, conv_weight, group_weight, slice_count, pooled_grad):
    vmem = pl.BlockSpec(memory_space=pltpu.VMEM)
    smem = pl.BlockSpec(memory_space=pltpu.SMEM)
    hbm = pl.BlockSpec(memory_space=pl.ANY)
    dma = pltpu.SemaphoreType.DMA
    conv, group = pl.pallas_call(
        kernel,
        out_shape=(
            jax.ShapeDtypeStruct((27, 16, 128), F32),
            jax.ShapeDtypeStruct((72, 16), F32),
        ),
        in_specs=[hbm, hbm, vmem, smem, vmem],
        out_specs=(vmem, vmem),
        scratch_shapes=[
            pltpu.VMEM((4, 1024, 128), BF16),
            pltpu.VMEM((3, 1152, 256), BF16),
            pltpu.VMEM((4, 272, 1280), BF16),
            pltpu.VMEM((384, 256), BF16),
            pltpu.VMEM((2, 256, 256), BF16),
            pltpu.VMEM((9, 256, 256), BF16),
            pltpu.VMEM((3, 288, 256), BF16),
            pltpu.VMEM((3, 288, 256), BF16),
            pltpu.VMEM((2, 128, 256), BF16),
            pltpu.VMEM((2, 128, 128), BF16),
            pltpu.VMEM((128, 256), BF16),
            pltpu.VMEM((128, 128), BF16),
            pltpu.VMEM((16, 2, 128, 128), BF16),
            pltpu.VMEM((16, 2, 128, 128), BF16),
            pltpu.VMEM((8, 2, 16, 128), F32),
            pltpu.VMEM((8, 2, 16, 128), F32),
            pltpu.VMEM((2, 16, 128), F32),
            pltpu.VMEM((16, 2, 16, 128), F32),
            dma((2,)),
            dma((3,)),
            dma((3,)),
            dma((2,)),
            dma((2,)),
            dma((16,)),
            dma((16,)),
            dma((8,)),
            dma((8,)),
            dma((16,)),
            dma((16,)),
        ],
        compiler_params=pltpu.CompilerParams(
            collective_id=0, has_side_effects=True, vmem_limit_bytes=40 * 1024 * 1024
        ),
        cost_estimate=pl.CostEstimate(
            flops=2_500_000_000, bytes_accessed=3_000_000, transcendentals=0
        ),
    )(
        volume.reshape(1024, 128),
        conv_weight.reshape(3, 1152, 256),
        group_weight.reshape(9, 8, 256),
        slice_count,
        pooled_grad,
    )
    conv = conv.reshape(3, 3, 3, 16, 128).swapaxes(3, 4)
    return conv, group.reshape(3, 3, 8, 16)


def solution(mesh):
    in_specs = (P("vol", "sp", None, None, None), P(), P(), P("vol"), P("vol", None))
    out_specs = (P(None, None, None, None, "sp"), P(None, None, None, "sp"))
    return jax.shard_map(local, mesh=mesh, in_specs=in_specs, out_specs=out_specs, check_vma=False)
```

```python
import jax
import jax.numpy as jnp
from jax import lax
from jax.experimental import pallas as pl
from jax.experimental.pallas import tpu as pltpu
from jax.sharding import PartitionSpec as P

BF16 = jnp.bfloat16
F32 = jnp.float32
CHUNKS = 4
Z_FIRST = ((5, 9), (5, 9), (6, 9))
VOL_NEAR_LAST = sorted(
    ((i, j) for i in range(4) for j in range(4) if i + j > 0),
    key=lambda o: -(min(o[0], 4 - o[0]) + min(o[1], 4 - o[1])),
)
Z_NEAR_LAST = (4, 3, 5, 2, 6, 1, 7)
Z_BLOCKS = 11


def remote(src, dst, send, recv, device):
    return pltpu.make_async_remote_copy(
        src_ref=src,
        dst_ref=dst,
        send_sem=send,
        recv_sem=recv,
        device_id=device,
        device_id_type=pl.DeviceIdType.MESH,
    )


def dot(left, right):
    return jnp.dot(left, right, preferred_element_type=F32)


def dot_nt(left, right):
    return lax.dot_general(left, right, (((1,), (1,)), ((), ())), preferred_element_type=F32)


def one_where(condition):
    return jnp.where(condition, 1.0, 0.0).astype(BF16)


def iota(shape, dim):
    return lax.broadcasted_iota(jnp.int32, shape, dim)


def kernel(
    vol,
    w,
    gw_hbm,
    cnt,
    pg_hbm,
    conv_out,
    group_out,
    volb,
    wv,
    gw,
    pg,
    xs,
    pick,
    shift,
    wg,
    hk,
    dk,
    dts,
    ggs,
    dx,
    gx,
    za,
    zr,
    ga,
    gr,
    va,
    vr,
    s2,
    r2,
    b2,
    rb2,
    f3,
    outb,
    loc_sem,
    sib_send,
    sib_recv,
    far_send,
    far_recv,
    dx_send,
    dx_recv,
    za_send,
    za_recv,
    ga_send,
    ga_recv,
    va_send,
    va_recv,
    s2_send,
    s2_recv,
    b2_send,
    b2_recv,
    f3_send,
    f3_recv,
):
    v = lax.axis_index("vol")
    sp = lax.axis_index("sp")
    x, y = lax.div(v, 4), lax.rem(v, 4)
    z, core = lax.div(sp, 2), lax.rem(sp, 2)
    sib = (v, z * 2 + 1 - core)
    far = (v, lax.rem(sp + 15 + 2 * core, 16))
    vol_peers = [lax.rem(x + i, 4) * 4 + lax.rem(y + j, 4) for i, j in VOL_NEAR_LAST]
    z_peers = [lax.rem(z + i, 8) for i in Z_NEAR_LAST]

    def at_z(k):
        return (v, k * 2 + core)

    own_copy = pltpu.make_async_copy(vol, volb.at[1 + core], loc_sem.at[0])
    own_copy.start()
    gw_copy = pltpu.make_async_copy(gw_hbm, gw, loc_sem.at[2])
    gw_copy.start()
    pg_copy = pltpu.make_async_copy(pg_hbm, pg, loc_sem.at[3])
    pg_copy.start()
    w_copy = pltpu.make_async_copy(w, wv, loc_sem.at[1])
    w_copy.start()

    barrier = pltpu.get_barrier_semaphore()
    for device in [sib, far] + [(k, sp) for k in vol_peers] + [at_z(k) for k in z_peers]:
        pl.semaphore_signal(barrier, inc=1, device_id=device, device_id_type=pl.DeviceIdType.MESH)

    m = iota((384, 256), 0)
    tap, within = lax.div(m, 128), lax.rem(m, 128)
    row = 2 * lax.div(lax.rem(within, 64), 16) + lax.div(within, 64)
    col = 2 * lax.rem(within, 16) + tap - 1
    pick[...] = one_where((iota((384, 256), 1) == row * 32 + col) & (col >= 0))

    pl.semaphore_wait(barrier, 24)

    def rows_of(chunk):
        return pl.ds(256 * chunk, 256)

    to_far = [
        remote(
            vol.at[rows_of(q)],
            volb.at[3 - 3 * core, rows_of(q)],
            far_send.at[q],
            far_recv.at[q],
            far,
        )
        for q in range(CHUNKS)
    ]
    to_sib = remote(vol, volb.at[1 + core], sib_send.at[0], sib_recv.at[0], sib)
    for copy in to_far:
        copy.start()
    to_sib.start()

    m, n = iota((256, 256), 0), iota((256, 256), 1)
    in_row = lax.rem(m, 16)
    shift[0] = one_where((n == m - 1) & (in_row != 0))
    shift[1] = one_where((n == m + 1) & (in_row != 15))
    same_group = lax.div(m, 8) == lax.div(n, 8)
    for k in range(3):
        hk[k, 0:16, :] = jnp.zeros((16, 256), BF16)
        hk[k, 272:288, :] = jnp.zeros((16, 256), BF16)
        dk[k, 0:16, :] = jnp.zeros((16, 256), BF16)
        dk[k, 272:288, :] = jnp.zeros((16, 256), BF16)

    def windows(slot, block, inside):
        if block == 0:
            xs[slot, 0:16, 0:384] = jnp.zeros((16, 384), BF16)
        picked = dot(pick[...], volb[slot, 256 * block : 256 * block + 256, :])
        if inside is not None:
            picked = picked * inside
        picked = picked.astype(BF16)
        for e in range(3):
            even = picked[e * 128 : e * 128 + 64]
            odd = picked[e * 128 + 64 : e * 128 + 128]
            for b, rows, offset in ((0, odd, 16), (1, even, 0), (2, odd, 0)):
                lane = (b * 3 + e) * 128
                start = 64 * block + offset
                xs[slot, start : start + 64, lane : lane + 128] = rows

    at_low = jnp.where(z == 0, 0.0, 1.0)
    at_high = jnp.where(z == 7, 0.0, 1.0)
    far_inside = jnp.where(core == 0, at_low, at_high)
    beyond_inside = jnp.where(core == 0, at_high, at_low)

    own_copy.wait()
    for block in range(4):
        windows(1 + core, block, None)
    gw_copy.wait()
    for jk in range(9):
        tiled = jnp.broadcast_to(gw[jk].astype(F32)[None], (32, 8, 256)).reshape(256, 256)
        wg[jk] = jnp.where(same_group, tiled, 0.0).astype(BF16)
    remote(vol, volb.at[2 - core], sib_send.at[0], sib_recv.at[0], sib).wait_recv()
    for block in range(4):
        windows(2 - core, block, None)
    w_copy.wait()
    pre = dot(xs[core + 1, 0:256, :], wv[1]) + dot(xs[2 - core, 0:256, :], wv[2 - 2 * core])
    for block in range(4):
        remote(
            vol.at[rows_of(block)],
            volb.at[3 * core, rows_of(block)],
            far_send.at[block],
            far_recv.at[block],
            far,
        ).wait_recv()
        windows(3 * core, block, far_inside)
    relay = remote(volb.at[3 * core], volb.at[3 * core], sib_send.at[1], sib_recv.at[1], sib)
    relay.start()
    pre = pre + dot(xs[3 * core, 0:256, :], wv[2 * core])

    pg_copy.wait()
    count = cnt[0]
    live = jnp.where(sp < count, 1.0, 0.0)
    hidden = (jnp.maximum(pre, 0.0) * live).astype(BF16)
    hk[1, 16:272, :] = hidden
    hk[0, 16:272, :] = dot(shift[0], hidden).astype(BF16)
    hk[2, 16:272, :] = dot(shift[1], hidden).astype(BF16)
    summed = hidden.astype(F32)
    for j in range(3):
        for k in range(3):
            summed = summed + dot(hk[k, 16 * j : 16 * j + 256, :], wg[3 * j + k])
    scale = 1.0 / jnp.full((1, 256), count.astype(F32) * 256.0)
    cotangent = pg[...] * live * scale
    d_wide = jnp.where(summed > 0, cotangent, 0.0)
    d_summed = d_wide.astype(BF16)
    dk[1, 16:272, :] = d_summed
    dk[0, 16:272, :] = dot(shift[0], d_summed).astype(BF16)
    dk[2, 16:272, :] = dot(shift[1], d_summed).astype(BF16)
    d_hidden = d_summed.astype(F32)
    for j in range(3):
        for k in range(3):
            lines = dk[2 - k, 16 * (2 - j) : 16 * (2 - j) + 256, :]
            d_hidden = d_hidden + dot_nt(lines, wg[3 * j + k])
    d_pre = jnp.where(pre > 0, d_hidden, 0.0) * live
    turned = d_pre.T.astype(BF16)
    for t in range(8):
        for c in range(2):
            start = 16 * (2 * t + c)
            dts[c, 16 * t : 16 * t + 16, :] = turned[start : start + 16, :]
    swap_d = remote(dts.at[1 - core], dx, dx_send.at[0], dx_recv.at[0], sib)
    swap_d.start()

    remote(
        volb.at[3 - 3 * core], volb.at[3 - 3 * core], sib_send.at[1], sib_recv.at[1], sib
    ).wait_recv()
    for block in range(4):
        windows(3 - 3 * core, block, beyond_inside)
    swap_d.wait_recv()

    def partial(a, first, end):
        lanes = slice(128 * first, 128 * end)
        total = dot(dts[core], xs[core + a, 0:256, lanes])
        return (total + dot(dx[...], xs[1 - core + a, 0:256, lanes])).astype(BF16)

    place = 0
    for a in range(3):
        first, end = Z_FIRST[a]
        total = partial(a, first, end)
        for q in range(end - first):
            for t in range(8):
                za[t, place + q] = total[16 * t : 16 * t + 16, 128 * q : 128 * q + 128]
        place += end - first
    z_sends = [
        remote(za.at[k], zr.at[z], za_send.at[k], za_recv.at[z], at_z(k)) for k in z_peers
    ]
    for copy in z_sends:
        copy.start()

    place = 0
    for a in range(3):
        first = Z_FIRST[a][0]
        total = partial(a, 0, first)
        for q in range(first):
            va[place + q] = total[:, 128 * q : 128 * q + 128]
        place += first
    v_sends = [
        remote(va.at[k], vr.at[v], va_send.at[k], va_recv.at[v], (k, sp)) for k in vol_peers
    ]
    for copy in v_sends:
        copy.start()

    d_turned = d_wide.T.astype(BF16)
    fold = one_where(lax.rem(iota((256, 128), 0), 8) == lax.rem(iota((256, 128), 1), 8))
    lane_tap = lax.div(iota((256, 128), 1), 8)
    grouped = jnp.zeros((256, 128), F32)
    for j in range(3):
        for k in range(3):
            full = dot(d_turned, hk[k, 16 * j : 16 * j + 256, :])
            kept = jnp.where(same_group, full, 0.0).astype(BF16)
            grouped = jnp.where(lane_tap == 3 * j + k, dot(kept, fold), grouped)
    grouped = grouped.astype(BF16)
    for t in range(8):
        for c in range(2):
            start = 16 * (2 * t + c)
            ggs[c, t] = grouped[start : start + 16, :]
    swap_g = remote(ggs.at[1 - core], gx, dx_send.at[1], dx_recv.at[1], sib)
    swap_g.start()
    swap_g.wait_recv()
    ga[...] = (ggs[core].astype(F32) + gx[...].astype(F32)).astype(BF16)
    g_sends = [
        remote(ga.at[k], gr.at[z], ga_send.at[k], ga_recv.at[z], at_z(k)) for k in z_peers
    ]
    for copy in g_sends:
        copy.start()

    total = va[v].astype(F32)
    for k in reversed(vol_peers):
        remote(va.at[0], vr.at[k], va_send.at[0], va_recv.at[k], (k, sp)).wait_recv()
        total = total + vr[k].astype(F32)
    for t in range(8):
        s2[t] = total[16 * t : 16 * t + 16, :]
    s2_sends = [
        remote(s2.at[k], r2.at[z], s2_send.at[k], s2_recv.at[z], at_z(k)) for k in z_peers
    ]
    for copy in s2_sends:
        copy.start()

    total = za[z].astype(F32)
    for k in reversed(z_peers):
        remote(za.at[0], zr.at[k], za_send.at[0], za_recv.at[k], at_z(k)).wait_recv()
        total = total + zr[k].astype(F32)
    b2[0:Z_BLOCKS] = total
    total = ga[z].astype(F32)
    for k in reversed(z_peers):
        remote(ga.at[0], gr.at[k], ga_send.at[0], ga_recv.at[k], at_z(k)).wait_recv()
        total = total + gr[k].astype(F32)
    b2[Z_BLOCKS] = total
    for k in vol_peers:

        @pl.when(k <= Z_BLOCKS)
        def _(k=k):
            remote(b2.at[k], rb2.at[v], b2_send.at[k], b2_recv.at[v], (k, sp)).start()

    total = s2[z]
    for k in reversed(z_peers):
        remote(s2.at[0], r2.at[k], s2_send.at[0], s2_recv.at[k], at_z(k)).wait_recv()
        total = total + r2[k]
    f3[0] = total
    outb[v, 0] = total

    @pl.when(v <= Z_BLOCKS)
    def _():
        total = b2[v]
        for k in reversed(vol_peers):
            remote(b2.at[0], rb2.at[k], b2_send.at[0], b2_recv.at[k], (k, sp)).wait_recv()
            total = total + rb2[k]
        f3[1] = total
        outb[v, 1] = total
        for k in vol_peers:
            remote(f3, outb.at[v], f3_send.at[k], f3_recv.at[v], (k, sp)).start()

    @pl.when(v > Z_BLOCKS)
    def _():
        for k in vol_peers:
            remote(f3.at[0], outb.at[v, 0], f3_send.at[k], f3_recv.at[v], (k, sp)).start()

    for k in reversed(vol_peers):

        @pl.when(k <= Z_BLOCKS)
        def _(k=k):
            remote(f3, outb.at[k], f3_send.at[0], f3_recv.at[k], (k, sp)).wait_recv()

        @pl.when(k > Z_BLOCKS)
        def _(k=k):
            remote(f3.at[0], outb.at[k, 0], f3_send.at[0], f3_recv.at[k], (k, sp)).wait_recv()

    by_vol, by_z = 0, 0
    for a in range(3):
        first, end = Z_FIRST[a]
        for t in range(first):
            conv_out[9 * a + t] = outb[by_vol, 0]
            by_vol += 1
        for t in range(first, end):
            conv_out[9 * a + t] = outb[by_z, 1]
            by_z += 1
    last = jnp.concatenate([outb[Z_BLOCKS, 1], jnp.zeros((112, 128), F32)], axis=0)
    group_out[...] = last.T[0:72, 0:16]

    for copy in to_far + [to_sib, relay, swap_d, swap_g] + z_sends + v_sends + g_sends + s2_sends:
        copy.wait_send()
    for k in vol_peers:

        @pl.when(k <= Z_BLOCKS)
        def _(k=k):
            remote(b2.at[k], rb2.at[v], b2_send.at[k], b2_recv.at[v], (k, sp)).wait_send()

        @pl.when(v <= Z_BLOCKS)
        def _(k=k):
            remote(f3, outb.at[v], f3_send.at[k], f3_recv.at[v], (k, sp)).wait_send()

        @pl.when(v > Z_BLOCKS)
        def _(k=k):
            remote(f3.at[0], outb.at[v, 0], f3_send.at[k], f3_recv.at[v], (k, sp)).wait_send()


def local(volume, conv_weight, group_weight, slice_count, pooled_grad):
    vmem = pl.BlockSpec(memory_space=pltpu.VMEM)
    smem = pl.BlockSpec(memory_space=pltpu.SMEM)
    hbm = pl.BlockSpec(memory_space=pltpu.HBM)
    dma = pltpu.SemaphoreType.DMA
    conv, group = pl.pallas_call(
        kernel,
        out_shape=(
            jax.ShapeDtypeStruct((27, 16, 128), F32),
            jax.ShapeDtypeStruct((72, 16), F32),
        ),
        in_specs=[hbm, hbm, hbm, smem, hbm],
        out_specs=(vmem, vmem),
        scratch_shapes=[
            pltpu.VMEM((4, 1024, 128), BF16),
            pltpu.VMEM((3, 1152, 256), BF16),
            pltpu.VMEM((9, 8, 256), BF16),
            pltpu.VMEM((1, 256), F32),
            pltpu.VMEM((4, 272, 1152), BF16),
            pltpu.VMEM((384, 256), BF16),
            pltpu.VMEM((2, 256, 256), BF16),
            pltpu.VMEM((9, 256, 256), BF16),
            pltpu.VMEM((3, 288, 256), BF16),
            pltpu.VMEM((3, 288, 256), BF16),
            pltpu.VMEM((2, 128, 256), BF16),
            pltpu.VMEM((2, 8, 16, 128), BF16),
            pltpu.VMEM((128, 256), BF16),
            pltpu.VMEM((8, 16, 128), BF16),
            pltpu.VMEM((8, Z_BLOCKS, 16, 128), BF16),
            pltpu.VMEM((8, Z_BLOCKS, 16, 128), BF16),
            pltpu.VMEM((8, 16, 128), BF16),
            pltpu.VMEM((8, 16, 128), BF16),
            pltpu.VMEM((16, 128, 128), BF16),
            pltpu.VMEM((16, 128, 128), BF16),
            pltpu.VMEM((8, 16, 128), F32),
            pltpu.VMEM((8, 16, 128), F32),
            pltpu.VMEM((Z_BLOCKS + 1, 16, 128), F32),
            pltpu.VMEM((16, 16, 128), F32),
            pltpu.VMEM((2, 16, 128), F32),
            pltpu.VMEM((16, 2, 16, 128), F32),
            dma((4,)),
            dma((2,)),
            dma((2,)),
            dma((CHUNKS,)),
            dma((CHUNKS,)),
            dma((2,)),
            dma((2,)),
            dma((8,)),
            dma((8,)),
            dma((8,)),
            dma((8,)),
            dma((16,)),
            dma((16,)),
            dma((8,)),
            dma((8,)),
            dma((16,)),
            dma((16,)),
            dma((16,)),
            dma((16,)),
        ],
        compiler_params=pltpu.CompilerParams(
            collective_id=0, has_side_effects=True, vmem_limit_bytes=56_000_000
        ),
        cost_estimate=pl.CostEstimate(
            flops=2_500_000_000, bytes_accessed=3_000_000, transcendentals=0
        ),
    )(
        volume.reshape(1024, 128),
        conv_weight.reshape(3, 1152, 256),
        group_weight.reshape(9, 8, 256),
        slice_count,
        pooled_grad,
    )
    conv = conv.reshape(3, 3, 3, 16, 128).swapaxes(3, 4)
    return conv, group.reshape(3, 3, 8, 16)


def solution(mesh):
    in_specs = (P("vol", "sp", None, None, None), P(), P(), P("vol"), P("vol", None))
    out_specs = (P(None, None, None, None, "sp"), P(None, None, None, "sp"))
    return jax.shard_map(local, mesh=mesh, in_specs=in_specs, out_specs=out_specs, check_vma=False)
```

```python
import jax
import jax.numpy as jnp
from jax import lax
from jax.experimental import pallas as pl
from jax.experimental.pallas import tpu as pltpu
from jax.sharding import PartitionSpec as P

BF16 = jnp.bfloat16
F32 = jnp.float32
CHUNKS = 4
Z_FIRST = ((5, 9), (5, 9), (6, 9))
VOL_NEAR_LAST = sorted(
    ((i, j) for i in range(4) for j in range(4) if i + j > 0),
    key=lambda o: -(min(o[0], 4 - o[0]) + min(o[1], 4 - o[1])),
)
Z_NEAR_LAST = (4, 3, 5, 2, 6, 1, 7)
Z_BLOCKS = 11


def remote(src, dst, send, recv, device):
    return pltpu.make_async_remote_copy(
        src_ref=src,
        dst_ref=dst,
        send_sem=send,
        recv_sem=recv,
        device_id=device,
        device_id_type=pl.DeviceIdType.MESH,
    )


def dot(left, right):
    return jnp.dot(left, right, preferred_element_type=F32)


def dot_nt(left, right):
    return lax.dot_general(left, right, (((1,), (1,)), ((), ())), preferred_element_type=F32)


def one_where(condition):
    return jnp.where(condition, 1.0, 0.0).astype(BF16)


def iota(shape, dim):
    return lax.broadcasted_iota(jnp.int32, shape, dim)


def kernel(
    vol,
    w,
    gw_hbm,
    cnt,
    pg_hbm,
    conv_out,
    group_out,
    volb,
    wv,
    gw,
    pg,
    xs,
    pick,
    shift,
    wg,
    hk,
    dk,
    dts,
    ggs,
    dx,
    gx,
    za,
    zr,
    zm,
    ga,
    gr,
    va,
    vr,
    s2,
    r2,
    b2,
    rb2,
    f3,
    outb,
    loc_sem,
    sib_send,
    sib_recv,
    relay_send,
    relay_recv,
    far_send,
    far_recv,
    dx_send,
    dx_recv,
    za_send,
    za_recv,
    zm_send,
    zm_recv,
    ga_send,
    ga_recv,
    va_send,
    va_recv,
    s2_send,
    s2_recv,
    b2_send,
    b2_recv,
    f3_send,
    f3_recv,
):
    v = lax.axis_index("vol")
    sp = lax.axis_index("sp")
    x, y = lax.div(v, 4), lax.rem(v, 4)
    z, core = lax.div(sp, 2), lax.rem(sp, 2)
    sib = (v, z * 2 + 1 - core)
    far = (v, lax.rem(sp + 15 + 2 * core, 16))
    vol_peers = [lax.rem(x + i, 4) * 4 + lax.rem(y + j, 4) for i, j in VOL_NEAR_LAST]
    z_peers = [lax.rem(z + i, 8) for i in Z_NEAR_LAST]

    def at_z(k):
        return (v, k * 2 + core)

    def along(places):
        return lax.rem(z + 8 + (1 - 2 * core) * places, 8)

    own_copy = pltpu.make_async_copy(vol, volb.at[1 + core], loc_sem.at[0])
    own_copy.start()
    gw_copy = pltpu.make_async_copy(gw_hbm, gw, loc_sem.at[2])
    gw_copy.start()
    pg_copy = pltpu.make_async_copy(pg_hbm, pg, loc_sem.at[3])
    pg_copy.start()
    w_copy = pltpu.make_async_copy(w, wv, loc_sem.at[1])
    w_copy.start()

    barrier = pltpu.get_barrier_semaphore()
    for device in [sib, far] + [(k, sp) for k in vol_peers] + [at_z(k) for k in z_peers]:
        pl.semaphore_signal(barrier, inc=1, device_id=device, device_id_type=pl.DeviceIdType.MESH)

    m = iota((384, 256), 0)
    tap, within = lax.div(m, 128), lax.rem(m, 128)
    row = 2 * lax.div(lax.rem(within, 64), 16) + lax.div(within, 64)
    col = 2 * lax.rem(within, 16) + tap - 1
    pick[...] = one_where((iota((384, 256), 1) == row * 32 + col) & (col >= 0))

    pl.semaphore_wait(barrier, 24)

    def rows_of(chunk):
        return pl.ds(256 * chunk, 256)

    to_far = [
        remote(
            vol.at[rows_of(q)],
            volb.at[3 - 3 * core, rows_of(q)],
            far_send.at[q],
            far_recv.at[q],
            far,
        )
        for q in range(CHUNKS)
    ]
    to_sib = remote(vol, volb.at[1 + core], sib_send.at[0], sib_recv.at[0], sib)
    for copy in to_far:
        copy.start()
    to_sib.start()

    m, n = iota((256, 256), 0), iota((256, 256), 1)
    in_row = lax.rem(m, 16)
    shift[0] = one_where((n == m - 1) & (in_row != 0))
    shift[1] = one_where((n == m + 1) & (in_row != 15))
    same_group = lax.div(m, 8) == lax.div(n, 8)
    for k in range(3):
        hk[k, 0:16, :] = jnp.zeros((16, 256), BF16)
        hk[k, 272:288, :] = jnp.zeros((16, 256), BF16)
        dk[k, 0:16, :] = jnp.zeros((16, 256), BF16)
        dk[k, 272:288, :] = jnp.zeros((16, 256), BF16)

    def windows(slot, block, inside):
        if block == 0:
            xs[slot, 0:16, 0:384] = jnp.zeros((16, 384), BF16)
        picked = dot(pick[...], volb[slot, 256 * block : 256 * block + 256, :])
        if inside is not None:
            picked = picked * inside
        picked = picked.astype(BF16)
        for e in range(3):
            even = picked[e * 128 : e * 128 + 64]
            odd = picked[e * 128 + 64 : e * 128 + 128]
            for b, rows, offset in ((0, odd, 16), (1, even, 0), (2, odd, 0)):
                lane = (b * 3 + e) * 128
                start = 64 * block + offset
                xs[slot, start : start + 64, lane : lane + 128] = rows

    at_low = jnp.where(z == 0, 0.0, 1.0)
    at_high = jnp.where(z == 7, 0.0, 1.0)
    far_inside = jnp.where(core == 0, at_low, at_high)
    beyond_inside = jnp.where(core == 0, at_high, at_low)

    own_copy.wait()
    for block in range(4):
        windows(1 + core, block, None)
    gw_copy.wait()
    for jk in range(9):
        tiled = jnp.broadcast_to(gw[jk].astype(F32)[None], (32, 8, 256)).reshape(256, 256)
        wg[jk] = jnp.where(same_group, tiled, 0.0).astype(BF16)
    remote(vol, volb.at[2 - core], sib_send.at[0], sib_recv.at[0], sib).wait_recv()
    for block in range(4):
        windows(2 - core, block, None)
    w_copy.wait()
    pre = dot(xs[core + 1, 0:256, :], wv[1]) + dot(xs[2 - core, 0:256, :], wv[2 - 2 * core])
    relays = []
    for block in range(4):
        remote(
            vol.at[rows_of(block)],
            volb.at[3 * core, rows_of(block)],
            far_send.at[block],
            far_recv.at[block],
            far,
        ).wait_recv()
        relay = remote(
            volb.at[3 * core, rows_of(block)],
            volb.at[3 * core, rows_of(block)],
            relay_send.at[block],
            relay_recv.at[block],
            sib,
        )
        relay.start()
        relays.append(relay)
        windows(3 * core, block, far_inside)
    pre = pre + dot(xs[3 * core, 0:256, :], wv[2 * core])

    pg_copy.wait()
    count = cnt[0]
    live = jnp.where(sp < count, 1.0, 0.0)
    hidden = (jnp.maximum(pre, 0.0) * live).astype(BF16)
    hk[1, 16:272, :] = hidden
    hk[0, 16:272, :] = dot(shift[0], hidden).astype(BF16)
    hk[2, 16:272, :] = dot(shift[1], hidden).astype(BF16)
    summed = hidden.astype(F32)
    for j in range(3):
        for k in range(3):
            summed = summed + dot(hk[k, 16 * j : 16 * j + 256, :], wg[3 * j + k])
    scale = 1.0 / jnp.full((1, 256), count.astype(F32) * 256.0)
    cotangent = pg[...] * live * scale
    d_wide = jnp.where(summed > 0, cotangent, 0.0)
    d_summed = d_wide.astype(BF16)
    dk[1, 16:272, :] = d_summed
    dk[0, 16:272, :] = dot(shift[0], d_summed).astype(BF16)
    dk[2, 16:272, :] = dot(shift[1], d_summed).astype(BF16)
    d_hidden = d_summed.astype(F32)
    for j in range(3):
        for k in range(3):
            lines = dk[2 - k, 16 * (2 - j) : 16 * (2 - j) + 256, :]
            d_hidden = d_hidden + dot_nt(lines, wg[3 * j + k])
    d_pre = jnp.where(pre > 0, d_hidden, 0.0) * live
    turned = d_pre.T.astype(BF16)
    for t in range(8):
        for c in range(2):
            start = 16 * (2 * t + c)
            dts[c, 16 * t : 16 * t + 16, :] = turned[start : start + 16, :]
    swap_d = remote(dts.at[1 - core], dx, dx_send.at[0], dx_recv.at[0], sib)
    swap_d.start()

    for block in range(4):
        remote(
            volb.at[3 - 3 * core, rows_of(block)],
            volb.at[3 - 3 * core, rows_of(block)],
            relay_send.at[block],
            relay_recv.at[block],
            sib,
        ).wait_recv()
        windows(3 - 3 * core, block, beyond_inside)
    swap_d.wait_recv()

    def partial(a, first, end):
        lanes = slice(128 * first, 128 * end)
        total = dot(dts[core], xs[core + a, 0:256, lanes])
        return (total + dot(dx[...], xs[1 - core + a, 0:256, lanes])).astype(BF16)

    place = 0
    for a in range(3):
        first, end = Z_FIRST[a]
        total = partial(a, first, end)
        for q in range(end - first):
            for t in range(8):
                za[t, place + q] = total[16 * t : 16 * t + 16, 128 * q : 128 * q + 128]
        place += end - first
    z_sends = [
        remote(
            za.at[along(home)], zm.at[i], zm_send.at[i], zm_recv.at[i], at_z(along(stop))
        )
        for i, (home, stop) in enumerate(((4, 2), (3, 1), (-3, -1)))
    ] + [
        remote(za.at[along(o)], zr.at[i], za_send.at[i], za_recv.at[i], at_z(along(o)))
        for i, o in enumerate((1, -1, 2, -2))
    ]
    for copy in z_sends[:5]:
        copy.start()

    place = 0
    for a in range(3):
        first = Z_FIRST[a][0]
        total = partial(a, 0, first)
        for q in range(first):
            va[place + q] = total[:, 128 * q : 128 * q + 128]
        place += first
    v_sends = [
        remote(va.at[k], vr.at[v], va_send.at[k], va_recv.at[v], (k, sp)) for k in vol_peers
    ]
    for copy in v_sends:
        copy.start()

    d_turned = d_wide.T.astype(BF16)
    fold = one_where(lax.rem(iota((256, 128), 0), 8) == lax.rem(iota((256, 128), 1), 8))
    lane_tap = lax.div(iota((256, 128), 1), 8)
    grouped = jnp.zeros((256, 128), F32)
    for j in range(3):
        for k in range(3):
            full = dot(d_turned, hk[k, 16 * j : 16 * j + 256, :])
            kept = jnp.where(same_group, full, 0.0).astype(BF16)
            grouped = jnp.where(lane_tap == 3 * j + k, dot(kept, fold), grouped)
    grouped = grouped.astype(BF16)
    for t in range(8):
        for c in range(2):
            start = 16 * (2 * t + c)
            ggs[c, t] = grouped[start : start + 16, :]
    swap_g = remote(ggs.at[1 - core], gx, dx_send.at[1], dx_recv.at[1], sib)
    swap_g.start()
    swap_g.wait_recv()
    ga[...] = (ggs[core].astype(F32) + gx[...].astype(F32)).astype(BF16)
    g_sends = [
        remote(ga.at[k], gr.at[z], ga_send.at[k], ga_recv.at[z], at_z(k)) for k in z_peers
    ]
    for copy in g_sends:
        copy.start()

    for copy in z_sends[:3]:
        copy.wait_recv()
    za[along(2)] = (za[along(2)].astype(F32) + zm[0].astype(F32) + zm[1].astype(F32)).astype(BF16)
    za[along(-2)] = (za[along(-2)].astype(F32) + zm[2].astype(F32)).astype(BF16)
    for copy in z_sends[5:]:
        copy.start()

    total = va[v].astype(F32)
    for k in reversed(vol_peers):
        remote(va.at[0], vr.at[k], va_send.at[0], va_recv.at[k], (k, sp)).wait_recv()
        total = total + vr[k].astype(F32)
    for t in range(8):
        s2[t] = total[16 * t : 16 * t + 16, :].astype(BF16)
    s2_sends = [
        remote(s2.at[k], r2.at[z], s2_send.at[k], s2_recv.at[z], at_z(k)) for k in z_peers
    ]
    for copy in s2_sends:
        copy.start()

    total = za[z].astype(F32)
    for i in range(4):
        z_sends[3 + i].wait_recv()
        total = total + zr[i].astype(F32)
    b2[0:Z_BLOCKS] = total.astype(BF16)
    total = ga[z].astype(F32)
    for k in reversed(z_peers):
        remote(ga.at[0], gr.at[k], ga_send.at[0], ga_recv.at[k], at_z(k)).wait_recv()
        total = total + gr[k].astype(F32)
    b2[Z_BLOCKS] = total.astype(BF16)
    for k in vol_peers:

        @pl.when(k <= Z_BLOCKS)
        def _(k=k):
            remote(b2.at[k], rb2.at[v], b2_send.at[k], b2_recv.at[v], (k, sp)).start()

    total = s2[z].astype(F32)
    for k in reversed(z_peers):
        remote(s2.at[0], r2.at[k], s2_send.at[0], s2_recv.at[k], at_z(k)).wait_recv()
        total = total + r2[k].astype(F32)
    f3[0] = total.astype(BF16)
    outb[v, 0] = total.astype(BF16)

    @pl.when(v <= Z_BLOCKS)
    def _():
        total = b2[v].astype(F32)
        for k in reversed(vol_peers):
            remote(b2.at[0], rb2.at[k], b2_send.at[0], b2_recv.at[k], (k, sp)).wait_recv()
            total = total + rb2[k].astype(F32)
        f3[1] = total.astype(BF16)
        outb[v, 1] = total.astype(BF16)
        for k in vol_peers:
            remote(f3, outb.at[v], f3_send.at[k], f3_recv.at[v], (k, sp)).start()

    @pl.when(v > Z_BLOCKS)
    def _():
        for k in vol_peers:
            remote(f3.at[0], outb.at[v, 0], f3_send.at[k], f3_recv.at[v], (k, sp)).start()

    for k in reversed(vol_peers):

        @pl.when(k <= Z_BLOCKS)
        def _(k=k):
            remote(f3, outb.at[k], f3_send.at[0], f3_recv.at[k], (k, sp)).wait_recv()

        @pl.when(k > Z_BLOCKS)
        def _(k=k):
            remote(f3.at[0], outb.at[k, 0], f3_send.at[0], f3_recv.at[k], (k, sp)).wait_recv()

    by_vol, by_z = 0, 0
    for a in range(3):
        first, end = Z_FIRST[a]
        for t in range(first):
            conv_out[9 * a + t] = outb[by_vol, 0].astype(F32)
            by_vol += 1
        for t in range(first, end):
            conv_out[9 * a + t] = outb[by_z, 1].astype(F32)
            by_z += 1
    last = jnp.concatenate([outb[Z_BLOCKS, 1].astype(F32), jnp.zeros((112, 128), F32)], axis=0)
    group_out[...] = last.T[0:72, 0:16]

    for copy in to_far + relays + [to_sib, swap_d, swap_g] + z_sends + v_sends + g_sends + s2_sends:
        copy.wait_send()
    for k in vol_peers:

        @pl.when(k <= Z_BLOCKS)
        def _(k=k):
            remote(b2.at[k], rb2.at[v], b2_send.at[k], b2_recv.at[v], (k, sp)).wait_send()

        @pl.when(v <= Z_BLOCKS)
        def _(k=k):
            remote(f3, outb.at[v], f3_send.at[k], f3_recv.at[v], (k, sp)).wait_send()

        @pl.when(v > Z_BLOCKS)
        def _(k=k):
            remote(f3.at[0], outb.at[v, 0], f3_send.at[k], f3_recv.at[v], (k, sp)).wait_send()


def local(volume, conv_weight, group_weight, slice_count, pooled_grad):
    vmem = pl.BlockSpec(memory_space=pltpu.VMEM)
    smem = pl.BlockSpec(memory_space=pltpu.SMEM)
    hbm = pl.BlockSpec(memory_space=pltpu.HBM)
    dma = pltpu.SemaphoreType.DMA
    conv, group = pl.pallas_call(
        kernel,
        out_shape=(
            jax.ShapeDtypeStruct((27, 16, 128), F32),
            jax.ShapeDtypeStruct((72, 16), F32),
        ),
        in_specs=[hbm, hbm, hbm, smem, hbm],
        out_specs=(vmem, vmem),
        scratch_shapes=[
            pltpu.VMEM((4, 1024, 128), BF16),
            pltpu.VMEM((3, 1152, 256), BF16),
            pltpu.VMEM((9, 8, 256), BF16),
            pltpu.VMEM((1, 256), F32),
            pltpu.VMEM((4, 272, 1152), BF16),
            pltpu.VMEM((384, 256), BF16),
            pltpu.VMEM((2, 256, 256), BF16),
            pltpu.VMEM((9, 256, 256), BF16),
            pltpu.VMEM((3, 288, 256), BF16),
            pltpu.VMEM((3, 288, 256), BF16),
            pltpu.VMEM((2, 128, 256), BF16),
            pltpu.VMEM((2, 8, 16, 128), BF16),
            pltpu.VMEM((128, 256), BF16),
            pltpu.VMEM((8, 16, 128), BF16),
            pltpu.VMEM((8, Z_BLOCKS, 16, 128), BF16),
            pltpu.VMEM((4, Z_BLOCKS, 16, 128), BF16),
            pltpu.VMEM((3, Z_BLOCKS, 16, 128), BF16),
            pltpu.VMEM((8, 16, 128), BF16),
            pltpu.VMEM((8, 16, 128), BF16),
            pltpu.VMEM((16, 128, 128), BF16),
            pltpu.VMEM((16, 128, 128), BF16),
            pltpu.VMEM((8, 16, 128), BF16),
            pltpu.VMEM((8, 16, 128), BF16),
            pltpu.VMEM((Z_BLOCKS + 1, 16, 128), BF16),
            pltpu.VMEM((16, 16, 128), BF16),
            pltpu.VMEM((2, 16, 128), BF16),
            pltpu.VMEM((16, 2, 16, 128), BF16),
            dma((4,)),
            dma((1,)),
            dma((1,)),
            dma((CHUNKS,)),
            dma((CHUNKS,)),
            dma((CHUNKS,)),
            dma((CHUNKS,)),
            dma((2,)),
            dma((2,)),
            dma((4,)),
            dma((4,)),
            dma((3,)),
            dma((3,)),
            dma((8,)),
            dma((8,)),
            dma((16,)),
            dma((16,)),
            dma((8,)),
            dma((8,)),
            dma((16,)),
            dma((16,)),
            dma((16,)),
            dma((16,)),
        ],
        compiler_params=pltpu.CompilerParams(
            collective_id=0, has_side_effects=True, vmem_limit_bytes=56_000_000
        ),
        cost_estimate=pl.CostEstimate(
            flops=2_500_000_000, bytes_accessed=3_000_000, transcendentals=0
        ),
    )(
        volume.reshape(1024, 128),
        conv_weight.reshape(3, 1152, 256),
        group_weight.reshape(9, 8, 256),
        slice_count,
        pooled_grad,
    )
    conv = conv.reshape(3, 3, 3, 16, 128).swapaxes(3, 4)
    return conv, group.reshape(3, 3, 8, 16)


def solution(mesh):
    in_specs = (P("vol", "sp", None, None, None), P(), P(), P("vol"), P("vol", None))
    out_specs = (P(None, None, None, None, "sp"), P(None, None, None, "sp"))
    return jax.shard_map(local, mesh=mesh, in_specs=in_specs, out_specs=out_specs, check_vma=False)
```

```python
import jax
import jax.numpy as jnp
from jax import lax
from jax.experimental import pallas as pl
from jax.experimental.pallas import tpu as pltpu
from jax.sharding import PartitionSpec as P

BF16 = jnp.bfloat16
F32 = jnp.float32
CHUNKS = 4
Z_FIRST = ((5, 9), (5, 9), (6, 9))
VOL_NEAR_LAST = sorted(
    ((i, j) for i in range(4) for j in range(4) if i + j > 0),
    key=lambda o: -(min(o[0], 4 - o[0]) + min(o[1], 4 - o[1])),
)
Z_NEAR_LAST = (4, 3, 5, 2, 6, 1, 7)
Z_BLOCKS = 11


def remote(src, dst, send, recv, device):
    return pltpu.make_async_remote_copy(
        src_ref=src,
        dst_ref=dst,
        send_sem=send,
        recv_sem=recv,
        device_id=device,
        device_id_type=pl.DeviceIdType.MESH,
    )


def dot(left, right):
    return jnp.dot(left, right, preferred_element_type=F32)


def dot_nt(left, right):
    return lax.dot_general(left, right, (((1,), (1,)), ((), ())), preferred_element_type=F32)


def one_where(condition):
    return jnp.where(condition, 1.0, 0.0).astype(BF16)


def iota(shape, dim):
    return lax.broadcasted_iota(jnp.int32, shape, dim)


def kernel(
    vol,
    w,
    gw_hbm,
    cnt,
    pg_hbm,
    conv_out,
    group_out,
    volb,
    wv,
    gw,
    pg,
    xs,
    pick,
    shift,
    wg,
    hk,
    dk,
    dts,
    ggs,
    dx,
    gx,
    za,
    zr,
    zm,
    ga,
    gr,
    va,
    vr,
    s2,
    r2,
    b2,
    rb2,
    f3,
    outb,
    round_sem,
    loc_sem,
    sib_send,
    sib_recv,
    relay_send,
    relay_recv,
    far_send,
    far_recv,
    dx_send,
    dx_recv,
    za_send,
    za_recv,
    zm_send,
    zm_recv,
    ga_send,
    ga_recv,
    va_send,
    va_recv,
    s2_send,
    s2_recv,
    b2_send,
    b2_recv,
    f3_send,
    f3_recv,
):
    v = lax.axis_index("vol")
    sp = lax.axis_index("sp")
    x, y = lax.div(v, 4), lax.rem(v, 4)
    z, core = lax.div(sp, 2), lax.rem(sp, 2)
    sib = (v, z * 2 + 1 - core)
    far = (v, lax.rem(sp + 15 + 2 * core, 16))
    vol_peers = [lax.rem(x + i, 4) * 4 + lax.rem(y + j, 4) for i, j in VOL_NEAR_LAST]
    z_peers = [lax.rem(z + i, 8) for i in Z_NEAR_LAST]

    def at_z(k):
        return (v, k * 2 + core)

    def along(places):
        return lax.rem(z + 8 + (1 - 2 * core) * places, 8)

    own_copy = pltpu.make_async_copy(vol, volb.at[1 + core], loc_sem.at[0])
    own_copy.start()
    gw_copy = pltpu.make_async_copy(gw_hbm, gw, loc_sem.at[2])
    gw_copy.start()
    pg_copy = pltpu.make_async_copy(pg_hbm, pg, loc_sem.at[3])
    pg_copy.start()
    w_copy = pltpu.make_async_copy(w, wv, loc_sem.at[1])
    w_copy.start()

    nearest = [
        (lax.rem(x + 1, 4) * 4 + y, sp),
        (lax.rem(x + 3, 4) * 4 + y, sp),
        (x * 4 + lax.rem(y + 1, 4), sp),
        (x * 4 + lax.rem(y + 3, 4), sp),
        at_z(lax.rem(z + 1, 8)),
        at_z(lax.rem(z + 7, 8)),
    ]
    barrier = pltpu.get_barrier_semaphore()
    for device in [sib, far] + nearest:
        pl.semaphore_signal(barrier, inc=1, device_id=device, device_id_type=pl.DeviceIdType.MESH)

    def tell(i):
        for device in nearest:
            pl.semaphore_signal(
                round_sem.at[i], inc=1, device_id=device, device_id_type=pl.DeviceIdType.MESH
            )

    def hear(i):
        pl.semaphore_wait(round_sem.at[i], len(nearest))

    m = iota((384, 256), 0)
    tap, within = lax.div(m, 128), lax.rem(m, 128)
    row = 2 * lax.div(lax.rem(within, 64), 16) + lax.div(within, 64)
    col = 2 * lax.rem(within, 16) + tap - 1
    pick[...] = one_where((iota((384, 256), 1) == row * 32 + col) & (col >= 0))

    pl.semaphore_wait(barrier, 2 + len(nearest))

    def rows_of(chunk):
        return pl.ds(256 * chunk, 256)

    to_far = [
        remote(
            vol.at[rows_of(q)],
            volb.at[3 - 3 * core, rows_of(q)],
            far_send.at[q],
            far_recv.at[q],
            far,
        )
        for q in range(CHUNKS)
    ]
    to_sib = remote(vol, volb.at[1 + core], sib_send.at[0], sib_recv.at[0], sib)
    for copy in to_far:
        copy.start()
    to_sib.start()
    tell(0)

    m, n = iota((256, 256), 0), iota((256, 256), 1)
    in_row = lax.rem(m, 16)
    shift[0] = one_where((n == m - 1) & (in_row != 0))
    shift[1] = one_where((n == m + 1) & (in_row != 15))
    same_group = lax.div(m, 8) == lax.div(n, 8)
    for k in range(3):
        hk[k, 0:16, :] = jnp.zeros((16, 256), BF16)
        hk[k, 272:288, :] = jnp.zeros((16, 256), BF16)
        dk[k, 0:16, :] = jnp.zeros((16, 256), BF16)
        dk[k, 272:288, :] = jnp.zeros((16, 256), BF16)

    def windows(slot, block, inside):
        if block == 0:
            xs[slot, 0:16, 0:384] = jnp.zeros((16, 384), BF16)
        picked = dot(pick[...], volb[slot, 256 * block : 256 * block + 256, :])
        if inside is not None:
            picked = picked * inside
        picked = picked.astype(BF16)
        for e in range(3):
            even = picked[e * 128 : e * 128 + 64]
            odd = picked[e * 128 + 64 : e * 128 + 128]
            for b, rows, offset in ((0, odd, 16), (1, even, 0), (2, odd, 0)):
                lane = (b * 3 + e) * 128
                start = 64 * block + offset
                xs[slot, start : start + 64, lane : lane + 128] = rows

    at_low = jnp.where(z == 0, 0.0, 1.0)
    at_high = jnp.where(z == 7, 0.0, 1.0)
    far_inside = jnp.where(core == 0, at_low, at_high)
    beyond_inside = jnp.where(core == 0, at_high, at_low)

    own_copy.wait()
    for block in range(4):
        windows(1 + core, block, None)
    gw_copy.wait()
    for jk in range(9):
        tiled = jnp.broadcast_to(gw[jk].astype(F32)[None], (32, 8, 256)).reshape(256, 256)
        wg[jk] = jnp.where(same_group, tiled, 0.0).astype(BF16)
    remote(vol, volb.at[2 - core], sib_send.at[0], sib_recv.at[0], sib).wait_recv()
    for block in range(4):
        windows(2 - core, block, None)
    hear(0)
    tell(1)
    w_copy.wait()
    pre = dot(xs[core + 1, 0:256, :], wv[1]) + dot(xs[2 - core, 0:256, :], wv[2 - 2 * core])
    relays = []
    for block in range(4):
        remote(
            vol.at[rows_of(block)],
            volb.at[3 * core, rows_of(block)],
            far_send.at[block],
            far_recv.at[block],
            far,
        ).wait_recv()
        relay = remote(
            volb.at[3 * core, rows_of(block)],
            volb.at[3 * core, rows_of(block)],
            relay_send.at[block],
            relay_recv.at[block],
            sib,
        )
        relay.start()
        relays.append(relay)
        windows(3 * core, block, far_inside)
    pre = pre + dot(xs[3 * core, 0:256, :], wv[2 * core])

    hear(1)
    tell(2)
    pg_copy.wait()
    count = cnt[0]
    live = jnp.where(sp < count, 1.0, 0.0)
    hidden = (jnp.maximum(pre, 0.0) * live).astype(BF16)
    hk[1, 16:272, :] = hidden
    hk[0, 16:272, :] = dot(shift[0], hidden).astype(BF16)
    hk[2, 16:272, :] = dot(shift[1], hidden).astype(BF16)
    summed = hidden.astype(F32)
    for j in range(3):
        for k in range(3):
            summed = summed + dot(hk[k, 16 * j : 16 * j + 256, :], wg[3 * j + k])
    scale = 1.0 / jnp.full((1, 256), count.astype(F32) * 256.0)
    cotangent = pg[...] * live * scale
    d_wide = jnp.where(summed > 0, cotangent, 0.0)
    d_summed = d_wide.astype(BF16)
    dk[1, 16:272, :] = d_summed
    dk[0, 16:272, :] = dot(shift[0], d_summed).astype(BF16)
    dk[2, 16:272, :] = dot(shift[1], d_summed).astype(BF16)
    d_hidden = d_summed.astype(F32)
    for j in range(3):
        for k in range(3):
            lines = dk[2 - k, 16 * (2 - j) : 16 * (2 - j) + 256, :]
            d_hidden = d_hidden + dot_nt(lines, wg[3 * j + k])
    d_pre = jnp.where(pre > 0, d_hidden, 0.0) * live
    turned = d_pre.T.astype(BF16)
    for t in range(8):
        for c in range(2):
            start = 16 * (2 * t + c)
            dts[c, 16 * t : 16 * t + 16, :] = turned[start : start + 16, :]
    swap_d = remote(dts.at[1 - core], dx, dx_send.at[0], dx_recv.at[0], sib)
    swap_d.start()

    for block in range(4):
        remote(
            volb.at[3 - 3 * core, rows_of(block)],
            volb.at[3 - 3 * core, rows_of(block)],
            relay_send.at[block],
            relay_recv.at[block],
            sib,
        ).wait_recv()
        windows(3 - 3 * core, block, beyond_inside)
    swap_d.wait_recv()

    def partial(a, first, end):
        lanes = slice(128 * first, 128 * end)
        total = dot(dts[core], xs[core + a, 0:256, lanes])
        return (total + dot(dx[...], xs[1 - core + a, 0:256, lanes])).astype(BF16)

    place = 0
    for a in range(3):
        first, end = Z_FIRST[a]
        total = partial(a, first, end)
        for q in range(end - first):
            for t in range(8):
                za[t, place + q] = total[16 * t : 16 * t + 16, 128 * q : 128 * q + 128]
        place += end - first
    hear(2)
    z_sends = [
        remote(
            za.at[along(home)], zm.at[i], zm_send.at[i], zm_recv.at[i], at_z(along(stop))
        )
        for i, (home, stop) in enumerate(((4, 2), (3, 1), (-3, -1)))
    ] + [
        remote(za.at[along(o)], zr.at[i], za_send.at[i], za_recv.at[i], at_z(along(o)))
        for i, o in enumerate((1, -1, 2, -2))
    ]
    for copy in z_sends[:5]:
        copy.start()

    place = 0
    for a in range(3):
        first = Z_FIRST[a][0]
        total = partial(a, 0, first)
        for q in range(first):
            va[place + q] = total[:, 128 * q : 128 * q + 128]
        place += first
    v_sends = [
        remote(va.at[k], vr.at[v], va_send.at[k], va_recv.at[v], (k, sp)) for k in vol_peers
    ]
    for copy in v_sends:
        copy.start()

    d_turned = d_wide.T.astype(BF16)
    fold = one_where(lax.rem(iota((256, 128), 0), 8) == lax.rem(iota((256, 128), 1), 8))
    lane_tap = lax.div(iota((256, 128), 1), 8)
    grouped = jnp.zeros((256, 128), F32)
    for j in range(3):
        for k in range(3):
            full = dot(d_turned, hk[k, 16 * j : 16 * j + 256, :])
            kept = jnp.where(same_group, full, 0.0).astype(BF16)
            grouped = jnp.where(lane_tap == 3 * j + k, dot(kept, fold), grouped)
    grouped = grouped.astype(BF16)
    for t in range(8):
        for c in range(2):
            start = 16 * (2 * t + c)
            ggs[c, t] = grouped[start : start + 16, :]
    swap_g = remote(ggs.at[1 - core], gx, dx_send.at[1], dx_recv.at[1], sib)
    swap_g.start()
    swap_g.wait_recv()
    ga[...] = (ggs[core].astype(F32) + gx[...].astype(F32)).astype(BF16)
    g_sends = [
        remote(ga.at[k], gr.at[z], ga_send.at[k], ga_recv.at[z], at_z(k)) for k in z_peers
    ]
    for copy in g_sends:
        copy.start()

    for copy in z_sends[:3]:
        copy.wait_recv()
    za[along(2)] = (za[along(2)].astype(F32) + zm[0].astype(F32) + zm[1].astype(F32)).astype(BF16)
    za[along(-2)] = (za[along(-2)].astype(F32) + zm[2].astype(F32)).astype(BF16)
    for copy in z_sends[5:]:
        copy.start()

    total = va[v].astype(F32)
    for k in reversed(vol_peers):
        remote(va.at[0], vr.at[k], va_send.at[0], va_recv.at[k], (k, sp)).wait_recv()
        total = total + vr[k].astype(F32)
    for t in range(8):
        s2[t] = total[16 * t : 16 * t + 16, :].astype(BF16)
    s2_sends = [
        remote(s2.at[k], r2.at[z], s2_send.at[k], s2_recv.at[z], at_z(k)) for k in z_peers
    ]
    for copy in s2_sends:
        copy.start()

    total = za[z].astype(F32)
    for i in range(4):
        z_sends[3 + i].wait_recv()
        total = total + zr[i].astype(F32)
    b2[0:Z_BLOCKS] = total.astype(BF16)
    total = ga[z].astype(F32)
    for k in reversed(z_peers):
        remote(ga.at[0], gr.at[k], ga_send.at[0], ga_recv.at[k], at_z(k)).wait_recv()
        total = total + gr[k].astype(F32)
    b2[Z_BLOCKS] = total.astype(BF16)
    for k in vol_peers:

        @pl.when(k <= Z_BLOCKS)
        def _(k=k):
            remote(b2.at[k], rb2.at[v], b2_send.at[k], b2_recv.at[v], (k, sp)).start()

    total = s2[z].astype(F32)
    for k in reversed(z_peers):
        remote(s2.at[0], r2.at[k], s2_send.at[0], s2_recv.at[k], at_z(k)).wait_recv()
        total = total + r2[k].astype(F32)
    f3[0] = total.astype(BF16)
    outb[v, 0] = total.astype(BF16)

    @pl.when(v <= Z_BLOCKS)
    def _():
        total = b2[v].astype(F32)
        for k in reversed(vol_peers):
            remote(b2.at[0], rb2.at[k], b2_send.at[0], b2_recv.at[k], (k, sp)).wait_recv()
            total = total + rb2[k].astype(F32)
        f3[1] = total.astype(BF16)
        outb[v, 1] = total.astype(BF16)
        for k in vol_peers:
            remote(f3, outb.at[v], f3_send.at[k], f3_recv.at[v], (k, sp)).start()

    @pl.when(v > Z_BLOCKS)
    def _():
        for k in vol_peers:
            remote(f3.at[0], outb.at[v, 0], f3_send.at[k], f3_recv.at[v], (k, sp)).start()

    for k in reversed(vol_peers):

        @pl.when(k <= Z_BLOCKS)
        def _(k=k):
            remote(f3, outb.at[k], f3_send.at[0], f3_recv.at[k], (k, sp)).wait_recv()

        @pl.when(k > Z_BLOCKS)
        def _(k=k):
            remote(f3.at[0], outb.at[k, 0], f3_send.at[0], f3_recv.at[k], (k, sp)).wait_recv()

    by_vol, by_z = 0, 0
    for a in range(3):
        first, end = Z_FIRST[a]
        for t in range(first):
            conv_out[9 * a + t] = outb[by_vol, 0].astype(F32)
            by_vol += 1
        for t in range(first, end):
            conv_out[9 * a + t] = outb[by_z, 1].astype(F32)
            by_z += 1
    last = jnp.concatenate([outb[Z_BLOCKS, 1].astype(F32), jnp.zeros((112, 128), F32)], axis=0)
    group_out[...] = last.T[0:72, 0:16]

    for copy in to_far + relays + [to_sib, swap_d, swap_g] + z_sends + v_sends + g_sends + s2_sends:
        copy.wait_send()
    for k in vol_peers:

        @pl.when(k <= Z_BLOCKS)
        def _(k=k):
            remote(b2.at[k], rb2.at[v], b2_send.at[k], b2_recv.at[v], (k, sp)).wait_send()

        @pl.when(v <= Z_BLOCKS)
        def _(k=k):
            remote(f3, outb.at[v], f3_send.at[k], f3_recv.at[v], (k, sp)).wait_send()

        @pl.when(v > Z_BLOCKS)
        def _(k=k):
            remote(f3.at[0], outb.at[v, 0], f3_send.at[k], f3_recv.at[v], (k, sp)).wait_send()


def in_hbm(array):
    return pltpu.with_memory_space_constraint(array, pltpu.HBM)


def local(volume, conv_weight, group_weight, slice_count, pooled_grad):
    vmem = pl.BlockSpec(memory_space=pltpu.VMEM)
    smem = pl.BlockSpec(memory_space=pltpu.SMEM)
    hbm = pl.BlockSpec(memory_space=pltpu.HBM)
    dma = pltpu.SemaphoreType.DMA
    conv, group = pl.pallas_call(
        kernel,
        out_shape=(
            jax.ShapeDtypeStruct((27, 16, 128), F32),
            jax.ShapeDtypeStruct((72, 16), F32),
        ),
        in_specs=[hbm, hbm, hbm, smem, hbm],
        out_specs=(vmem, vmem),
        scratch_shapes=[
            pltpu.VMEM((4, 1024, 128), BF16),
            pltpu.VMEM((3, 1152, 256), BF16),
            pltpu.VMEM((9, 8, 256), BF16),
            pltpu.VMEM((1, 256), F32),
            pltpu.VMEM((4, 272, 1152), BF16),
            pltpu.VMEM((384, 256), BF16),
            pltpu.VMEM((2, 256, 256), BF16),
            pltpu.VMEM((9, 256, 256), BF16),
            pltpu.VMEM((3, 288, 256), BF16),
            pltpu.VMEM((3, 288, 256), BF16),
            pltpu.VMEM((2, 128, 256), BF16),
            pltpu.VMEM((2, 8, 16, 128), BF16),
            pltpu.VMEM((128, 256), BF16),
            pltpu.VMEM((8, 16, 128), BF16),
            pltpu.VMEM((8, Z_BLOCKS, 16, 128), BF16),
            pltpu.VMEM((4, Z_BLOCKS, 16, 128), BF16),
            pltpu.VMEM((3, Z_BLOCKS, 16, 128), BF16),
            pltpu.VMEM((8, 16, 128), BF16),
            pltpu.VMEM((8, 16, 128), BF16),
            pltpu.VMEM((16, 128, 128), BF16),
            pltpu.VMEM((16, 128, 128), BF16),
            pltpu.VMEM((8, 16, 128), BF16),
            pltpu.VMEM((8, 16, 128), BF16),
            pltpu.VMEM((Z_BLOCKS + 1, 16, 128), BF16),
            pltpu.VMEM((16, 16, 128), BF16),
            pltpu.VMEM((2, 16, 128), BF16),
            pltpu.VMEM((16, 2, 16, 128), BF16),
            pltpu.SemaphoreType.REGULAR((3,)),
            dma((4,)),
            dma((1,)),
            dma((1,)),
            dma((CHUNKS,)),
            dma((CHUNKS,)),
            dma((CHUNKS,)),
            dma((CHUNKS,)),
            dma((2,)),
            dma((2,)),
            dma((4,)),
            dma((4,)),
            dma((3,)),
            dma((3,)),
            dma((8,)),
            dma((8,)),
            dma((16,)),
            dma((16,)),
            dma((8,)),
            dma((8,)),
            dma((16,)),
            dma((16,)),
            dma((16,)),
            dma((16,)),
        ],
        compiler_params=pltpu.CompilerParams(
            collective_id=0, has_side_effects=True, vmem_limit_bytes=48_000_000
        ),
        cost_estimate=pl.CostEstimate(
            flops=2_500_000_000, bytes_accessed=3_000_000, transcendentals=0
        ),
    )(
        in_hbm(volume.reshape(1024, 128)),
        in_hbm(conv_weight.reshape(3, 1152, 256)),
        in_hbm(group_weight.reshape(9, 8, 256)),
        slice_count,
        in_hbm(pooled_grad),
    )
    conv = conv.reshape(3, 3, 3, 16, 128).swapaxes(3, 4)
    return conv, group.reshape(3, 3, 8, 16)


def solution(mesh):
    in_specs = (P("vol", "sp", None, None, None), P(), P(), P("vol"), P("vol", None))
    out_specs = (P(None, None, None, None, "sp"), P(None, None, None, "sp"))
    return jax.shard_map(local, mesh=mesh, in_specs=in_specs, out_specs=out_specs, check_vma=False)
```

```python
import jax
import jax.numpy as jnp
from jax import lax
from jax.experimental import pallas as pl
from jax.experimental.pallas import tpu as pltpu
from jax.sharding import PartitionSpec as P

BF16 = jnp.bfloat16
F32 = jnp.float32
CHUNKS = 4
Z_FIRST = ((5, 9), (5, 9), (6, 9))
VOL_NEAR_LAST = sorted(
    ((i, j) for i in range(4) for j in range(4) if i + j > 0),
    key=lambda o: -(min(o[0], 4 - o[0]) + min(o[1], 4 - o[1])),
)
Z_NEAR_LAST = (4, 3, 5, 2, 6, 1, 7)
Z_BLOCKS = 11


def remote(src, dst, send, recv, device):
    return pltpu.make_async_remote_copy(
        src_ref=src,
        dst_ref=dst,
        send_sem=send,
        recv_sem=recv,
        device_id=device,
        device_id_type=pl.DeviceIdType.MESH,
    )


def dot(left, right):
    return jnp.dot(left, right, preferred_element_type=F32)


def dot_nt(left, right):
    return lax.dot_general(left, right, (((1,), (1,)), ((), ())), preferred_element_type=F32)


def one_where(condition):
    return jnp.where(condition, 1.0, 0.0).astype(BF16)


def iota(shape, dim):
    return lax.broadcasted_iota(jnp.int32, shape, dim)


def kernel(
    vol,
    w,
    gw_hbm,
    cnt,
    pg_hbm,
    conv_out,
    group_out,
    volb,
    wv,
    gw,
    pg,
    xs,
    pick,
    shift,
    wg,
    hk,
    dk,
    dts,
    ggs,
    dx,
    gx,
    za,
    zr,
    zm,
    ga,
    gr,
    va,
    vr,
    s2,
    r2,
    b2,
    rb2,
    f3,
    outb,
    round_sem,
    loc_sem,
    sib_send,
    sib_recv,
    relay_send,
    relay_recv,
    far_send,
    far_recv,
    dx_send,
    dx_recv,
    za_send,
    za_recv,
    zm_send,
    zm_recv,
    ga_send,
    ga_recv,
    va_send,
    va_recv,
    s2_send,
    s2_recv,
    b2_send,
    b2_recv,
    f3_send,
    f3_recv,
):
    v = lax.axis_index("vol")
    sp = lax.axis_index("sp")
    x, y = lax.div(v, 4), lax.rem(v, 4)
    z, core = lax.div(sp, 2), lax.rem(sp, 2)
    sib = (v, z * 2 + 1 - core)
    far = (v, lax.rem(sp + 15 + 2 * core, 16))
    vol_peers = [lax.rem(x + i, 4) * 4 + lax.rem(y + j, 4) for i, j in VOL_NEAR_LAST]
    z_peers = [lax.rem(z + i, 8) for i in Z_NEAR_LAST]

    def at_z(k):
        return (v, k * 2 + core)

    def along(places):
        return lax.rem(z + 8 + (1 - 2 * core) * places, 8)

    own_copy = pltpu.make_async_copy(vol, volb.at[1 + core], loc_sem.at[0])
    own_copy.start()
    gw_copy = pltpu.make_async_copy(gw_hbm, gw, loc_sem.at[2])
    gw_copy.start()
    pg_copy = pltpu.make_async_copy(pg_hbm, pg, loc_sem.at[3])
    pg_copy.start()
    w_copy = pltpu.make_async_copy(w, wv, loc_sem.at[1])
    w_copy.start()

    nearest = [
        (lax.rem(x + 1, 4) * 4 + y, sp),
        (lax.rem(x + 3, 4) * 4 + y, sp),
        (x * 4 + lax.rem(y + 1, 4), sp),
        (x * 4 + lax.rem(y + 3, 4), sp),
        at_z(lax.rem(z + 1, 8)),
        at_z(lax.rem(z + 7, 8)),
    ]
    barrier = pltpu.get_barrier_semaphore()
    for device in [sib, far] + nearest:
        pl.semaphore_signal(barrier, inc=1, device_id=device, device_id_type=pl.DeviceIdType.MESH)

    def tell(i):
        for device in nearest:
            pl.semaphore_signal(
                round_sem.at[i], inc=1, device_id=device, device_id_type=pl.DeviceIdType.MESH
            )

    def hear(i):
        pl.semaphore_wait(round_sem.at[i], len(nearest))

    m = iota((384, 256), 0)
    tap, within = lax.div(m, 128), lax.rem(m, 128)
    row = 2 * lax.div(lax.rem(within, 64), 16) + lax.div(within, 64)
    col = 2 * lax.rem(within, 16) + tap - 1
    pick[...] = one_where((iota((384, 256), 1) == row * 32 + col) & (col >= 0))

    pl.semaphore_wait(barrier, 2 + len(nearest))

    def rows_of(chunk):
        return pl.ds(256 * chunk, 256)

    to_far = [
        remote(
            vol.at[rows_of(q)],
            volb.at[3 - 3 * core, rows_of(q)],
            far_send.at[q],
            far_recv.at[q],
            far,
        )
        for q in range(CHUNKS)
    ]
    to_sib = remote(vol, volb.at[1 + core], sib_send.at[0], sib_recv.at[0], sib)
    for copy in to_far:
        copy.start()
    to_sib.start()
    tell(0)

    m, n = iota((256, 256), 0), iota((256, 256), 1)
    in_row = lax.rem(m, 16)
    shift[0] = one_where((n == m - 1) & (in_row != 0))
    shift[1] = one_where((n == m + 1) & (in_row != 15))
    same_group = lax.div(m, 8) == lax.div(n, 8)
    for k in range(3):
        hk[k, 0:16, :] = jnp.zeros((16, 256), BF16)
        hk[k, 272:288, :] = jnp.zeros((16, 256), BF16)
        dk[k, 0:16, :] = jnp.zeros((16, 256), BF16)
        dk[k, 272:288, :] = jnp.zeros((16, 256), BF16)

    def windows(slot, block, inside):
        if block == 0:
            xs[slot, 0:16, 0:384] = jnp.zeros((16, 384), BF16)
        picked = dot(pick[...], volb[slot, 256 * block : 256 * block + 256, :])
        if inside is not None:
            picked = picked * inside
        picked = picked.astype(BF16)
        for e in range(3):
            even = picked[e * 128 : e * 128 + 64]
            odd = picked[e * 128 + 64 : e * 128 + 128]
            for b, rows, offset in ((0, odd, 16), (1, even, 0), (2, odd, 0)):
                lane = (b * 3 + e) * 128
                start = 64 * block + offset
                xs[slot, start : start + 64, lane : lane + 128] = rows

    at_low = jnp.where(z == 0, 0.0, 1.0)
    at_high = jnp.where(z == 7, 0.0, 1.0)
    far_inside = jnp.where(core == 0, at_low, at_high)
    beyond_inside = jnp.where(core == 0, at_high, at_low)

    own_copy.wait()
    for block in range(4):
        windows(1 + core, block, None)
    gw_copy.wait()
    for jk in range(9):
        tiled = jnp.broadcast_to(gw[jk].astype(F32)[None], (32, 8, 256)).reshape(256, 256)
        wg[jk] = jnp.where(same_group, tiled, 0.0).astype(BF16)
    remote(vol, volb.at[2 - core], sib_send.at[0], sib_recv.at[0], sib).wait_recv()
    for block in range(4):
        windows(2 - core, block, None)
    hear(0)
    tell(1)
    w_copy.wait()
    pre = dot(xs[core + 1, 0:256, :], wv[1]) + dot(xs[2 - core, 0:256, :], wv[2 - 2 * core])
    relays = []
    for block in range(4):
        remote(
            vol.at[rows_of(block)],
            volb.at[3 * core, rows_of(block)],
            far_send.at[block],
            far_recv.at[block],
            far,
        ).wait_recv()
        relay = remote(
            volb.at[3 * core, rows_of(block)],
            volb.at[3 * core, rows_of(block)],
            relay_send.at[block],
            relay_recv.at[block],
            sib,
        )
        relay.start()
        relays.append(relay)
        windows(3 * core, block, far_inside)
    pre = pre + dot(xs[3 * core, 0:256, :], wv[2 * core])

    hear(1)
    tell(2)
    pg_copy.wait()
    count = cnt[0]
    live = jnp.where(sp < count, 1.0, 0.0)
    hidden = (jnp.maximum(pre, 0.0) * live).astype(BF16)
    hk[1, 16:272, :] = hidden
    hk[0, 16:272, :] = dot(shift[0], hidden).astype(BF16)
    hk[2, 16:272, :] = dot(shift[1], hidden).astype(BF16)
    summed = hidden.astype(F32)
    for j in range(3):
        for k in range(3):
            summed = summed + dot(hk[k, 16 * j : 16 * j + 256, :], wg[3 * j + k])
    scale = 1.0 / jnp.full((1, 256), count.astype(F32) * 256.0)
    cotangent = pg[...] * live * scale
    d_wide = jnp.where(summed > 0, cotangent, 0.0)
    d_summed = d_wide.astype(BF16)
    dk[1, 16:272, :] = d_summed
    dk[0, 16:272, :] = dot(shift[0], d_summed).astype(BF16)
    dk[2, 16:272, :] = dot(shift[1], d_summed).astype(BF16)
    d_hidden = d_summed.astype(F32)
    for j in range(3):
        for k in range(3):
            lines = dk[2 - k, 16 * (2 - j) : 16 * (2 - j) + 256, :]
            d_hidden = d_hidden + dot_nt(lines, wg[3 * j + k])
    d_pre = jnp.where(pre > 0, d_hidden, 0.0) * live
    turned = d_pre.T.astype(BF16)
    for t in range(8):
        for c in range(2):
            start = 16 * (2 * t + c)
            dts[c, 16 * t : 16 * t + 16, :] = turned[start : start + 16, :]
    swap_d = remote(dts.at[1 - core], dx, dx_send.at[0], dx_recv.at[0], sib)
    swap_d.start()

    for block in range(4):
        remote(
            volb.at[3 - 3 * core, rows_of(block)],
            volb.at[3 - 3 * core, rows_of(block)],
            relay_send.at[block],
            relay_recv.at[block],
            sib,
        ).wait_recv()
        windows(3 - 3 * core, block, beyond_inside)
    swap_d.wait_recv()

    def partial(a, first, end):
        lanes = slice(128 * first, 128 * end)
        total = dot(dts[core], xs[core + a, 0:256, lanes])
        return (total + dot(dx[...], xs[1 - core + a, 0:256, lanes])).astype(BF16)

    place = 0
    for a in range(3):
        first, end = Z_FIRST[a]
        total = partial(a, first, end)
        for q in range(end - first):
            for t in range(8):
                za[t, place + q] = total[16 * t : 16 * t + 16, 128 * q : 128 * q + 128]
        place += end - first
    hear(2)
    z_sends = [
        remote(
            za.at[along(home)], zm.at[i], zm_send.at[i], zm_recv.at[i], at_z(along(stop))
        )
        for i, (home, stop) in enumerate(((4, 2), (3, 1), (-3, -1)))
    ] + [
        remote(za.at[along(o)], zr.at[i], za_send.at[i], za_recv.at[i], at_z(along(o)))
        for i, o in enumerate((1, -1, 2, -2))
    ]
    for copy in z_sends[:3]:
        copy.start()

    place = 0
    for a in range(3):
        first = Z_FIRST[a][0]
        total = partial(a, 0, first)
        for q in range(first):
            for h in range(2):
                va[h, place + q] = total[64 * h : 64 * h + 64, 128 * q : 128 * q + 128]
        place += first
    v_sends = [
        remote(va.at[h, k], vr.at[h, v], va_send.at[h, k], va_recv.at[h, v], (k, sp))
        for h in range(2)
        for k in vol_peers
    ]
    for copy in v_sends:
        copy.start()

    d_turned = d_wide.T.astype(BF16)
    fold = one_where(lax.rem(iota((256, 128), 0), 8) == lax.rem(iota((256, 128), 1), 8))
    lane_tap = lax.div(iota((256, 128), 1), 8)
    grouped = jnp.zeros((256, 128), F32)
    for j in range(3):
        for k in range(3):
            full = dot(d_turned, hk[k, 16 * j : 16 * j + 256, :])
            kept = jnp.where(same_group, full, 0.0).astype(BF16)
            grouped = jnp.where(lane_tap == 3 * j + k, dot(kept, fold), grouped)
    grouped = grouped.astype(BF16)
    for t in range(8):
        for c in range(2):
            start = 16 * (2 * t + c)
            ggs[c, t] = grouped[start : start + 16, :]
    swap_g = remote(ggs.at[1 - core], gx, dx_send.at[1], dx_recv.at[1], sib)
    swap_g.start()
    swap_g.wait_recv()
    ga[...] = (ggs[core].astype(F32) + gx[...].astype(F32)).astype(BF16)
    g_sends = [
        remote(ga.at[k], gr.at[z], ga_send.at[k], ga_recv.at[z], at_z(k)) for k in z_peers
    ]
    for copy in g_sends:
        copy.start()

    for copy in z_sends[3:5]:
        copy.start()
    for copy in z_sends[:3]:
        copy.wait_recv()
    za[along(2)] = (za[along(2)].astype(F32) + zm[0].astype(F32) + zm[1].astype(F32)).astype(BF16)
    za[along(-2)] = (za[along(-2)].astype(F32) + zm[2].astype(F32)).astype(BF16)
    for copy in z_sends[5:]:
        copy.start()

    def over_z(h):
        total = va[h, v].astype(F32)
        for k in reversed(vol_peers):
            remote(
                va.at[0, 0], vr.at[h, k], va_send.at[h, 0], va_recv.at[h, k], (k, sp)
            ).wait_recv()
            total = total + vr[h, k].astype(F32)
        for t in range(4):
            s2[4 * h + t] = total[16 * t : 16 * t + 16, :].astype(BF16)
        for copy, k in zip(s2_sends, z_peers):

            @pl.when(lax.div(k, 4) == h)
            def _(copy=copy):
                copy.start()

    s2_sends = [
        remote(s2.at[k], r2.at[z], s2_send.at[k], s2_recv.at[z], at_z(k)) for k in z_peers
    ]
    over_z(0)

    total = za[z].astype(F32)
    for i in range(4):
        z_sends[3 + i].wait_recv()
        total = total + zr[i].astype(F32)
    b2[0:Z_BLOCKS] = total.astype(BF16)
    total = ga[z].astype(F32)
    for k in reversed(z_peers):
        remote(ga.at[0], gr.at[k], ga_send.at[0], ga_recv.at[k], at_z(k)).wait_recv()
        total = total + gr[k].astype(F32)
    b2[Z_BLOCKS] = total.astype(BF16)
    for k in vol_peers:

        @pl.when(k <= Z_BLOCKS)
        def _(k=k):
            remote(b2.at[k], rb2.at[v], b2_send.at[k], b2_recv.at[v], (k, sp)).start()

    over_z(1)

    total = s2[z].astype(F32)
    for k in reversed(z_peers):
        remote(s2.at[0], r2.at[k], s2_send.at[0], s2_recv.at[k], at_z(k)).wait_recv()
        total = total + r2[k].astype(F32)
    f3[0] = total.astype(BF16)
    outb[v, 0] = total.astype(BF16)

    @pl.when(v <= Z_BLOCKS)
    def _():
        total = b2[v].astype(F32)
        for k in reversed(vol_peers):
            remote(b2.at[0], rb2.at[k], b2_send.at[0], b2_recv.at[k], (k, sp)).wait_recv()
            total = total + rb2[k].astype(F32)
        f3[1] = total.astype(BF16)
        outb[v, 1] = total.astype(BF16)
        for k in vol_peers:
            remote(f3, outb.at[v], f3_send.at[k], f3_recv.at[v], (k, sp)).start()

    @pl.when(v > Z_BLOCKS)
    def _():
        for k in vol_peers:
            remote(f3.at[0], outb.at[v, 0], f3_send.at[k], f3_recv.at[v], (k, sp)).start()

    for copy in to_far + relays + [to_sib, swap_d, swap_g] + z_sends + v_sends + g_sends + s2_sends:
        copy.wait_send()
    for k in vol_peers:

        @pl.when(k <= Z_BLOCKS)
        def _(k=k):
            remote(b2.at[k], rb2.at[v], b2_send.at[k], b2_recv.at[v], (k, sp)).wait_send()

    for k in reversed(vol_peers):

        @pl.when(k <= Z_BLOCKS)
        def _(k=k):
            remote(f3, outb.at[k], f3_send.at[0], f3_recv.at[k], (k, sp)).wait_recv()

        @pl.when(k > Z_BLOCKS)
        def _(k=k):
            remote(f3.at[0], outb.at[k, 0], f3_send.at[0], f3_recv.at[k], (k, sp)).wait_recv()

    by_vol, by_z = 0, 0
    for a in range(3):
        first, end = Z_FIRST[a]
        for t in range(first):
            conv_out[9 * a + t] = outb[by_vol, 0].astype(F32)
            by_vol += 1
        for t in range(first, end):
            conv_out[9 * a + t] = outb[by_z, 1].astype(F32)
            by_z += 1
    last = jnp.concatenate([outb[Z_BLOCKS, 1].astype(F32), jnp.zeros((112, 128), F32)], axis=0)
    group_out[...] = last.T[0:72, 0:16]

    @pl.when(v <= Z_BLOCKS)
    def _():
        for k in vol_peers:
            remote(f3, outb.at[v], f3_send.at[k], f3_recv.at[v], (k, sp)).wait_send()

    @pl.when(v > Z_BLOCKS)
    def _():
        for k in vol_peers:
            remote(f3.at[0], outb.at[v, 0], f3_send.at[k], f3_recv.at[v], (k, sp)).wait_send()


def in_hbm(array):
    return pltpu.with_memory_space_constraint(array, pltpu.HBM)


def local(volume, conv_weight, group_weight, slice_count, pooled_grad):
    vmem = pl.BlockSpec(memory_space=pltpu.VMEM)
    smem = pl.BlockSpec(memory_space=pltpu.SMEM)
    hbm = pl.BlockSpec(memory_space=pltpu.HBM)
    dma = pltpu.SemaphoreType.DMA
    conv, group = pl.pallas_call(
        kernel,
        out_shape=(
            jax.ShapeDtypeStruct((27, 16, 128), F32),
            jax.ShapeDtypeStruct((72, 16), F32),
        ),
        in_specs=[hbm, hbm, hbm, smem, hbm],
        out_specs=(vmem, vmem),
        scratch_shapes=[
            pltpu.VMEM((4, 1024, 128), BF16),
            pltpu.VMEM((3, 1152, 256), BF16),
            pltpu.VMEM((9, 8, 256), BF16),
            pltpu.VMEM((1, 256), F32),
            pltpu.VMEM((4, 272, 1152), BF16),
            pltpu.VMEM((384, 256), BF16),
            pltpu.VMEM((2, 256, 256), BF16),
            pltpu.VMEM((9, 256, 256), BF16),
            pltpu.VMEM((3, 288, 256), BF16),
            pltpu.VMEM((3, 288, 256), BF16),
            pltpu.VMEM((2, 128, 256), BF16),
            pltpu.VMEM((2, 8, 16, 128), BF16),
            pltpu.VMEM((128, 256), BF16),
            pltpu.VMEM((8, 16, 128), BF16),
            pltpu.VMEM((8, Z_BLOCKS, 16, 128), BF16),
            pltpu.VMEM((4, Z_BLOCKS, 16, 128), BF16),
            pltpu.VMEM((3, Z_BLOCKS, 16, 128), BF16),
            pltpu.VMEM((8, 16, 128), BF16),
            pltpu.VMEM((8, 16, 128), BF16),
            pltpu.VMEM((2, 16, 64, 128), BF16),
            pltpu.VMEM((2, 16, 64, 128), BF16),
            pltpu.VMEM((8, 16, 128), BF16),
            pltpu.VMEM((8, 16, 128), BF16),
            pltpu.VMEM((Z_BLOCKS + 1, 16, 128), BF16),
            pltpu.VMEM((16, 16, 128), BF16),
            pltpu.VMEM((2, 16, 128), BF16),
            pltpu.VMEM((16, 2, 16, 128), BF16),
            pltpu.SemaphoreType.REGULAR((3,)),
            dma((4,)),
            dma((1,)),
            dma((1,)),
            dma((CHUNKS,)),
            dma((CHUNKS,)),
            dma((CHUNKS,)),
            dma((CHUNKS,)),
            dma((2,)),
            dma((2,)),
            dma((4,)),
            dma((4,)),
            dma((3,)),
            dma((3,)),
            dma((8,)),
            dma((8,)),
            dma((2, 16)),
            dma((2, 16)),
            dma((8,)),
            dma((8,)),
            dma((16,)),
            dma((16,)),
            dma((16,)),
            dma((16,)),
        ],
        compiler_params=pltpu.CompilerParams(
            collective_id=0, has_side_effects=True, vmem_limit_bytes=48_000_000
        ),
        cost_estimate=pl.CostEstimate(
            flops=2_500_000_000, bytes_accessed=3_000_000, transcendentals=0
        ),
    )(
        in_hbm(volume.reshape(1024, 128)),
        in_hbm(conv_weight.reshape(3, 1152, 256)),
        in_hbm(group_weight.reshape(9, 8, 256)),
        slice_count,
        in_hbm(pooled_grad),
    )
    conv = conv.reshape(3, 3, 3, 16, 128).swapaxes(3, 4)
    return conv, group.reshape(3, 3, 8, 16)


def solution(mesh):
    in_specs = (P("vol", "sp", None, None, None), P(), P(), P("vol"), P("vol", None))
    out_specs = (P(None, None, None, None, "sp"), P(None, None, None, "sp"))
    return jax.shard_map(local, mesh=mesh, in_specs=in_specs, out_specs=out_specs, check_vma=False)
```

```python
import jax
import jax.numpy as jnp
from jax import lax
from jax.experimental import pallas as pl
from jax.experimental.pallas import tpu as pltpu
from jax.sharding import PartitionSpec as P

BF16 = jnp.bfloat16
F32 = jnp.float32
CHUNKS = 4
Z_FIRST = ((5, 9), (5, 9), (6, 9))
VOL_NEAR_LAST = sorted(
    ((i, j) for i in range(4) for j in range(4) if i + j > 0),
    key=lambda o: -(min(o[0], 4 - o[0]) + min(o[1], 4 - o[1])),
)
Z_NEAR_LAST = (4, 3, 5, 2, 6, 1, 7)
Z_BLOCKS = 11


def remote(src, dst, send, recv, device):
    return pltpu.make_async_remote_copy(
        src_ref=src,
        dst_ref=dst,
        send_sem=send,
        recv_sem=recv,
        device_id=device,
        device_id_type=pl.DeviceIdType.MESH,
    )


def dot(left, right):
    return jnp.dot(left, right, preferred_element_type=F32)


def dot_nt(left, right):
    return lax.dot_general(left, right, (((1,), (1,)), ((), ())), preferred_element_type=F32)


def one_where(condition):
    return jnp.where(condition, 1.0, 0.0).astype(BF16)


def iota(shape, dim):
    return lax.broadcasted_iota(jnp.int32, shape, dim)


def kernel(
    vol,
    w,
    gw_hbm,
    cnt,
    pg_hbm,
    conv_out,
    group_out,
    volb,
    wv,
    gw,
    pg,
    xs,
    pick,
    shift,
    wg,
    hk,
    dk,
    dts,
    ggs,
    dx,
    gx,
    za,
    zr,
    zm,
    ga,
    gr,
    va,
    vr,
    s2,
    r2,
    b2,
    rb2,
    f3,
    outb,
    round_sem,
    loc_sem,
    sib_send,
    sib_recv,
    relay_send,
    relay_recv,
    far_send,
    far_recv,
    dx_send,
    dx_recv,
    za_send,
    za_recv,
    zm_send,
    zm_recv,
    ga_send,
    ga_recv,
    va_send,
    va_recv,
    s2_send,
    s2_recv,
    b2_send,
    b2_recv,
    f3_send,
    f3_recv,
):
    v = lax.axis_index("vol")
    sp = lax.axis_index("sp")
    x, y = lax.div(v, 4), lax.rem(v, 4)
    z, core = lax.div(sp, 2), lax.rem(sp, 2)
    sib = (v, z * 2 + 1 - core)
    far = (v, lax.rem(sp + 15 + 2 * core, 16))
    vol_peers = [lax.rem(x + i, 4) * 4 + lax.rem(y + j, 4) for i, j in VOL_NEAR_LAST]
    z_peers = [lax.rem(z + i, 8) for i in Z_NEAR_LAST]

    def at_z(k):
        return (v, k * 2 + core)

    def along(places):
        return lax.rem(z + 8 + (1 - 2 * core) * places, 8)

    own_copy = pltpu.make_async_copy(vol, volb.at[1 + core], loc_sem.at[0])
    own_copy.start()
    gw_copy = pltpu.make_async_copy(gw_hbm, gw, loc_sem.at[2])
    gw_copy.start()
    pg_copy = pltpu.make_async_copy(pg_hbm, pg, loc_sem.at[3])
    pg_copy.start()
    w_copy = pltpu.make_async_copy(w, wv, loc_sem.at[1])
    w_copy.start()

    nearest = [
        (lax.rem(x + 1, 4) * 4 + y, sp),
        (lax.rem(x + 3, 4) * 4 + y, sp),
        (x * 4 + lax.rem(y + 1, 4), sp),
        (x * 4 + lax.rem(y + 3, 4), sp),
        at_z(lax.rem(z + 1, 8)),
        at_z(lax.rem(z + 7, 8)),
    ]
    barrier = pltpu.get_barrier_semaphore()
    for device in [sib, far] + nearest:
        pl.semaphore_signal(barrier, inc=1, device_id=device, device_id_type=pl.DeviceIdType.MESH)

    def tell(i):
        for device in nearest:
            pl.semaphore_signal(
                round_sem.at[i], inc=1, device_id=device, device_id_type=pl.DeviceIdType.MESH
            )

    def hear(i):
        pl.semaphore_wait(round_sem.at[i], len(nearest))

    m = iota((384, 256), 0)
    tap, within = lax.div(m, 128), lax.rem(m, 128)
    row = 2 * lax.div(lax.rem(within, 64), 16) + lax.div(within, 64)
    col = 2 * lax.rem(within, 16) + tap - 1
    pick[...] = one_where((iota((384, 256), 1) == row * 32 + col) & (col >= 0))

    pl.semaphore_wait(barrier, 2 + len(nearest))

    def rows_of(chunk):
        return pl.ds(256 * chunk, 256)

    to_far = [
        remote(
            vol.at[rows_of(q)],
            volb.at[3 - 3 * core, rows_of(q)],
            far_send.at[q],
            far_recv.at[q],
            far,
        )
        for q in range(CHUNKS)
    ]
    to_sib = remote(vol, volb.at[1 + core], sib_send.at[0], sib_recv.at[0], sib)
    for copy in to_far:
        copy.start()
    to_sib.start()
    tell(0)

    m, n = iota((256, 256), 0), iota((256, 256), 1)
    in_row = lax.rem(m, 16)
    shift[0] = one_where((n == m - 1) & (in_row != 0))
    shift[1] = one_where((n == m + 1) & (in_row != 15))
    same_group = lax.div(m, 8) == lax.div(n, 8)
    for k in range(3):
        hk[k, 0:16, :] = jnp.zeros((16, 256), BF16)
        hk[k, 272:288, :] = jnp.zeros((16, 256), BF16)
        dk[k, 0:16, :] = jnp.zeros((16, 256), BF16)
        dk[k, 272:288, :] = jnp.zeros((16, 256), BF16)

    def windows(slot, block, inside):
        if block == 0:
            xs[slot, 0:16, 0:384] = jnp.zeros((16, 384), BF16)
        picked = dot(pick[...], volb[slot, 256 * block : 256 * block + 256, :])
        if inside is not None:
            picked = picked * inside
        picked = picked.astype(BF16)
        for e in range(3):
            even = picked[e * 128 : e * 128 + 64]
            odd = picked[e * 128 + 64 : e * 128 + 128]
            for b, rows, offset in ((0, odd, 16), (1, even, 0), (2, odd, 0)):
                lane = (b * 3 + e) * 128
                start = 64 * block + offset
                xs[slot, start : start + 64, lane : lane + 128] = rows

    at_low = jnp.where(z == 0, 0.0, 1.0)
    at_high = jnp.where(z == 7, 0.0, 1.0)
    far_inside = jnp.where(core == 0, at_low, at_high)
    beyond_inside = jnp.where(core == 0, at_high, at_low)

    own_copy.wait()
    for block in range(4):
        windows(1 + core, block, None)
    gw_copy.wait()
    for jk in range(9):
        tiled = jnp.broadcast_to(gw[jk].astype(F32)[None], (32, 8, 256)).reshape(256, 256)
        wg[jk] = jnp.where(same_group, tiled, 0.0).astype(BF16)
    remote(vol, volb.at[2 - core], sib_send.at[0], sib_recv.at[0], sib).wait_recv()
    for block in range(4):
        windows(2 - core, block, None)
    hear(0)
    tell(1)
    w_copy.wait()
    pre = dot(xs[core + 1, 0:256, :], wv[1]) + dot(xs[2 - core, 0:256, :], wv[2 - 2 * core])
    relays = []
    for block in range(4):
        remote(
            vol.at[rows_of(block)],
            volb.at[3 * core, rows_of(block)],
            far_send.at[block],
            far_recv.at[block],
            far,
        ).wait_recv()
        relay = remote(
            volb.at[3 * core, rows_of(block)],
            volb.at[3 * core, rows_of(block)],
            relay_send.at[block],
            relay_recv.at[block],
            sib,
        )
        relay.start()
        relays.append(relay)
        windows(3 * core, block, far_inside)
    pre = pre + dot(xs[3 * core, 0:256, :], wv[2 * core])

    hear(1)
    tell(2)
    pg_copy.wait()
    count = cnt[0]
    live = jnp.where(sp < count, 1.0, 0.0)
    hidden = (jnp.maximum(pre, 0.0) * live).astype(BF16)
    hk[1, 16:272, :] = hidden
    hk[0, 16:272, :] = dot(shift[0], hidden).astype(BF16)
    hk[2, 16:272, :] = dot(shift[1], hidden).astype(BF16)
    summed = hidden.astype(F32)
    for j in range(3):
        for k in range(3):
            summed = summed + dot(hk[k, 16 * j : 16 * j + 256, :], wg[3 * j + k])
    scale = 1.0 / jnp.full((1, 256), count.astype(F32) * 256.0)
    cotangent = pg[...] * live * scale
    d_wide = jnp.where(summed > 0, cotangent, 0.0)
    d_summed = d_wide.astype(BF16)
    dk[1, 16:272, :] = d_summed
    dk[0, 16:272, :] = dot(shift[0], d_summed).astype(BF16)
    dk[2, 16:272, :] = dot(shift[1], d_summed).astype(BF16)
    d_hidden = d_summed.astype(F32)
    for j in range(3):
        for k in range(3):
            lines = dk[2 - k, 16 * (2 - j) : 16 * (2 - j) + 256, :]
            d_hidden = d_hidden + dot_nt(lines, wg[3 * j + k])
    d_pre = jnp.where(pre > 0, d_hidden, 0.0) * live
    turned = d_pre.T.astype(BF16)
    for t in range(8):
        for c in range(2):
            start = 16 * (2 * t + c)
            dts[c, 16 * t : 16 * t + 16, :] = turned[start : start + 16, :]
    swap_d = remote(dts.at[1 - core], dx, dx_send.at[0], dx_recv.at[0], sib)
    swap_d.start()

    for block in range(4):
        remote(
            volb.at[3 - 3 * core, rows_of(block)],
            volb.at[3 - 3 * core, rows_of(block)],
            relay_send.at[block],
            relay_recv.at[block],
            sib,
        ).wait_recv()
        windows(3 - 3 * core, block, beyond_inside)
    swap_d.wait_recv()

    def partial(a, first, end):
        lanes = slice(128 * first, 128 * end)
        total = dot(dts[core], xs[core + a, 0:256, lanes])
        return (total + dot(dx[...], xs[1 - core + a, 0:256, lanes])).astype(BF16)

    place = 0
    for a in range(3):
        first, end = Z_FIRST[a]
        total = partial(a, first, end)
        for q in range(end - first):
            for t in range(8):
                za[t, place + q] = total[16 * t : 16 * t + 16, 128 * q : 128 * q + 128]
        place += end - first
    hear(2)
    z_sends = [
        remote(
            za.at[along(home)], zm.at[i], zm_send.at[i], zm_recv.at[i], at_z(along(stop))
        )
        for i, (home, stop) in enumerate(((4, 2), (3, 1), (-3, -1)))
    ] + [
        remote(za.at[along(o)], zr.at[i], za_send.at[i], za_recv.at[i], at_z(along(o)))
        for i, o in enumerate((1, -1, 2, -2))
    ]
    for copy in z_sends[:3]:
        copy.start()

    place = 0
    for a in range(3):
        first = Z_FIRST[a][0]
        total = partial(a, 0, first)
        for q in range(first):
            for h in range(2):
                va[h, place + q] = total[64 * h : 64 * h + 64, 128 * q : 128 * q + 128]
        place += first
    v_sends = [
        remote(va.at[h, k], vr.at[h, v], va_send.at[h, k], va_recv.at[h, v], (k, sp))
        for h in range(2)
        for k in vol_peers
    ]
    for copy in v_sends[: len(vol_peers)]:
        copy.start()

    d_turned = d_wide.T.astype(BF16)
    fold = one_where(lax.rem(iota((256, 128), 0), 8) == lax.rem(iota((256, 128), 1), 8))
    lane_tap = lax.div(iota((256, 128), 1), 8)
    grouped = jnp.zeros((256, 128), F32)
    for j in range(3):
        for k in range(3):
            full = dot(d_turned, hk[k, 16 * j : 16 * j + 256, :])
            kept = jnp.where(same_group, full, 0.0).astype(BF16)
            grouped = jnp.where(lane_tap == 3 * j + k, dot(kept, fold), grouped)
    grouped = grouped.astype(BF16)
    for t in range(8):
        for c in range(2):
            start = 16 * (2 * t + c)
            ggs[c, t] = grouped[start : start + 16, :]
    swap_g = remote(ggs.at[1 - core], gx, dx_send.at[1], dx_recv.at[1], sib)
    swap_g.start()
    swap_g.wait_recv()
    ga[...] = (ggs[core].astype(F32) + gx[...].astype(F32)).astype(BF16)
    g_sends = [
        remote(ga.at[k], gr.at[z], ga_send.at[k], ga_recv.at[z], at_z(k)) for k in z_peers
    ]
    for copy in g_sends:
        copy.start()
    for copy in v_sends[len(vol_peers) :]:
        copy.start()

    for copy in z_sends[3:5]:
        copy.start()
    for copy in z_sends[:3]:
        copy.wait_recv()
    za[along(2)] = (za[along(2)].astype(F32) + zm[0].astype(F32) + zm[1].astype(F32)).astype(BF16)
    za[along(-2)] = (za[along(-2)].astype(F32) + zm[2].astype(F32)).astype(BF16)
    for copy in z_sends[5:]:
        copy.start()

    def over_z(h):
        total = va[h, v].astype(F32)
        for k in reversed(vol_peers):
            remote(
                va.at[0, 0], vr.at[h, k], va_send.at[h, 0], va_recv.at[h, k], (k, sp)
            ).wait_recv()
            total = total + vr[h, k].astype(F32)
        for t in range(4):
            s2[4 * h + t] = total[16 * t : 16 * t + 16, :].astype(BF16)
        for copy, k in zip(s2_sends, z_peers):

            @pl.when(lax.div(k, 4) == h)
            def _(copy=copy):
                copy.start()

    s2_sends = [
        remote(s2.at[k], r2.at[z], s2_send.at[k], s2_recv.at[z], at_z(k)) for k in z_peers
    ]
    over_z(0)

    total = za[z].astype(F32)
    for i in range(4):
        z_sends[3 + i].wait_recv()
        total = total + zr[i].astype(F32)
    b2[0:Z_BLOCKS] = total.astype(BF16)
    total = ga[z].astype(F32)
    for k in reversed(z_peers):
        remote(ga.at[0], gr.at[k], ga_send.at[0], ga_recv.at[k], at_z(k)).wait_recv()
        total = total + gr[k].astype(F32)
    b2[Z_BLOCKS] = total.astype(BF16)
    for k in vol_peers:

        @pl.when(k <= Z_BLOCKS)
        def _(k=k):
            remote(b2.at[k], rb2.at[v], b2_send.at[k], b2_recv.at[v], (k, sp)).start()

    over_z(1)

    total = s2[z].astype(F32)
    for k in reversed(z_peers):
        remote(s2.at[0], r2.at[k], s2_send.at[0], s2_recv.at[k], at_z(k)).wait_recv()
        total = total + r2[k].astype(F32)
    f3[0] = total.astype(BF16)
    outb[v, 0] = total.astype(BF16)

    @pl.when(v <= Z_BLOCKS)
    def _():
        total = b2[v].astype(F32)
        for k in reversed(vol_peers):
            remote(b2.at[0], rb2.at[k], b2_send.at[0], b2_recv.at[k], (k, sp)).wait_recv()
            total = total + rb2[k].astype(F32)
        f3[1] = total.astype(BF16)
        outb[v, 1] = total.astype(BF16)
        for k in vol_peers:
            remote(f3, outb.at[v], f3_send.at[k], f3_recv.at[v], (k, sp)).start()

    @pl.when(v > Z_BLOCKS)
    def _():
        for k in vol_peers:
            remote(f3.at[0], outb.at[v, 0], f3_send.at[k], f3_recv.at[v], (k, sp)).start()

    for copy in to_far + relays + [to_sib, swap_d, swap_g] + z_sends + v_sends + g_sends + s2_sends:
        copy.wait_send()
    for k in vol_peers:

        @pl.when(k <= Z_BLOCKS)
        def _(k=k):
            remote(b2.at[k], rb2.at[v], b2_send.at[k], b2_recv.at[v], (k, sp)).wait_send()

    for k in reversed(vol_peers):

        @pl.when(k <= Z_BLOCKS)
        def _(k=k):
            remote(f3, outb.at[k], f3_send.at[0], f3_recv.at[k], (k, sp)).wait_recv()

        @pl.when(k > Z_BLOCKS)
        def _(k=k):
            remote(f3.at[0], outb.at[k, 0], f3_send.at[0], f3_recv.at[k], (k, sp)).wait_recv()

    by_vol, by_z = 0, 0
    for a in range(3):
        first, end = Z_FIRST[a]
        for t in range(first):
            conv_out[9 * a + t] = outb[by_vol, 0].astype(F32)
            by_vol += 1
        for t in range(first, end):
            conv_out[9 * a + t] = outb[by_z, 1].astype(F32)
            by_z += 1
    last = jnp.concatenate([outb[Z_BLOCKS, 1].astype(F32), jnp.zeros((112, 128), F32)], axis=0)
    group_out[...] = last.T[0:72, 0:16]

    @pl.when(v <= Z_BLOCKS)
    def _():
        for k in vol_peers:
            remote(f3, outb.at[v], f3_send.at[k], f3_recv.at[v], (k, sp)).wait_send()

    @pl.when(v > Z_BLOCKS)
    def _():
        for k in vol_peers:
            remote(f3.at[0], outb.at[v, 0], f3_send.at[k], f3_recv.at[v], (k, sp)).wait_send()


def in_hbm(array):
    return pltpu.with_memory_space_constraint(array, pltpu.HBM)


def local(volume, conv_weight, group_weight, slice_count, pooled_grad):
    vmem = pl.BlockSpec(memory_space=pltpu.VMEM)
    smem = pl.BlockSpec(memory_space=pltpu.SMEM)
    hbm = pl.BlockSpec(memory_space=pltpu.HBM)
    dma = pltpu.SemaphoreType.DMA
    conv, group = pl.pallas_call(
        kernel,
        out_shape=(
            jax.ShapeDtypeStruct((27, 16, 128), F32),
            jax.ShapeDtypeStruct((72, 16), F32),
        ),
        in_specs=[hbm, hbm, hbm, smem, hbm],
        out_specs=(vmem, vmem),
        scratch_shapes=[
            pltpu.VMEM((4, 1024, 128), BF16),
            pltpu.VMEM((3, 1152, 256), BF16),
            pltpu.VMEM((9, 8, 256), BF16),
            pltpu.VMEM((1, 256), F32),
            pltpu.VMEM((4, 272, 1152), BF16),
            pltpu.VMEM((384, 256), BF16),
            pltpu.VMEM((2, 256, 256), BF16),
            pltpu.VMEM((9, 256, 256), BF16),
            pltpu.VMEM((3, 288, 256), BF16),
            pltpu.VMEM((3, 288, 256), BF16),
            pltpu.VMEM((2, 128, 256), BF16),
            pltpu.VMEM((2, 8, 16, 128), BF16),
            pltpu.VMEM((128, 256), BF16),
            pltpu.VMEM((8, 16, 128), BF16),
            pltpu.VMEM((8, Z_BLOCKS, 16, 128), BF16),
            pltpu.VMEM((4, Z_BLOCKS, 16, 128), BF16),
            pltpu.VMEM((3, Z_BLOCKS, 16, 128), BF16),
            pltpu.VMEM((8, 16, 128), BF16),
            pltpu.VMEM((8, 16, 128), BF16),
            pltpu.VMEM((2, 16, 64, 128), BF16),
            pltpu.VMEM((2, 16, 64, 128), BF16),
            pltpu.VMEM((8, 16, 128), BF16),
            pltpu.VMEM((8, 16, 128), BF16),
            pltpu.VMEM((Z_BLOCKS + 1, 16, 128), BF16),
            pltpu.VMEM((16, 16, 128), BF16),
            pltpu.VMEM((2, 16, 128), BF16),
            pltpu.VMEM((16, 2, 16, 128), BF16),
            pltpu.SemaphoreType.REGULAR((3,)),
            dma((4,)),
            dma((1,)),
            dma((1,)),
            dma((CHUNKS,)),
            dma((CHUNKS,)),
            dma((CHUNKS,)),
            dma((CHUNKS,)),
            dma((2,)),
            dma((2,)),
            dma((4,)),
            dma((4,)),
            dma((3,)),
            dma((3,)),
            dma((8,)),
            dma((8,)),
            dma((2, 16)),
            dma((2, 16)),
            dma((8,)),
            dma((8,)),
            dma((16,)),
            dma((16,)),
            dma((16,)),
            dma((16,)),
        ],
        compiler_params=pltpu.CompilerParams(
            collective_id=0, has_side_effects=True, vmem_limit_bytes=48_000_000
        ),
        cost_estimate=pl.CostEstimate(
            flops=2_500_000_000, bytes_accessed=3_000_000, transcendentals=0
        ),
    )(
        in_hbm(volume.reshape(1024, 128)),
        in_hbm(conv_weight.reshape(3, 1152, 256)),
        in_hbm(group_weight.reshape(9, 8, 256)),
        slice_count,
        in_hbm(pooled_grad),
    )
    conv = conv.reshape(3, 3, 3, 16, 128).swapaxes(3, 4)
    return conv, group.reshape(3, 3, 8, 16)


def solution(mesh):
    in_specs = (P("vol", "sp", None, None, None), P(), P(), P("vol"), P("vol", None))
    out_specs = (P(None, None, None, None, "sp"), P(None, None, None, "sp"))
    return jax.shard_map(local, mesh=mesh, in_specs=in_specs, out_specs=out_specs, check_vma=False)
```

```python
import jax
import jax.numpy as jnp
from jax import lax
from jax.experimental import pallas as pl
from jax.experimental.pallas import tpu as pltpu
from jax.sharding import PartitionSpec as P

BF16 = jnp.bfloat16
F32 = jnp.float32
CHUNKS = 4
Z_FIRST = ((5, 9), (5, 9), (6, 9))
VOL_NEAR_LAST = sorted(
    ((i, j) for i in range(4) for j in range(4) if i + j > 0),
    key=lambda o: -(min(o[0], 4 - o[0]) + min(o[1], 4 - o[1])),
)
Z_NEAR_LAST = (4, 3, 5, 2, 6, 1, 7)
Z_BLOCKS = 11


def remote(src, dst, send, recv, device):
    return pltpu.make_async_remote_copy(
        src_ref=src,
        dst_ref=dst,
        send_sem=send,
        recv_sem=recv,
        device_id=device,
        device_id_type=pl.DeviceIdType.MESH,
    )


def dot(left, right):
    return jnp.dot(left, right, preferred_element_type=F32)


def dot_nt(left, right):
    return lax.dot_general(left, right, (((1,), (1,)), ((), ())), preferred_element_type=F32)


def one_where(condition):
    return jnp.where(condition, 1.0, 0.0).astype(BF16)


def iota(shape, dim):
    return lax.broadcasted_iota(jnp.int32, shape, dim)


def kernel(
    vol,
    w,
    gw_hbm,
    cnt,
    pg_hbm,
    conv_out,
    group_out,
    volb,
    wv,
    gw,
    pg,
    xs,
    pick,
    shift,
    wg,
    hk,
    dk,
    dts,
    ggs,
    dx,
    gx,
    za,
    zr,
    zm,
    ga,
    gr,
    va,
    vr,
    s2,
    r2,
    b2,
    rb2,
    f3,
    outb,
    round_sem,
    loc_sem,
    sib_send,
    sib_recv,
    relay_send,
    relay_recv,
    far_send,
    far_recv,
    dx_send,
    dx_recv,
    za_send,
    za_recv,
    zm_send,
    zm_recv,
    ga_send,
    ga_recv,
    va_send,
    va_recv,
    s2_send,
    s2_recv,
    b2_send,
    b2_recv,
    f3_send,
    f3_recv,
):
    v = lax.axis_index("vol")
    sp = lax.axis_index("sp")
    x, y = lax.div(v, 4), lax.rem(v, 4)
    z, core = lax.div(sp, 2), lax.rem(sp, 2)
    sib = (v, z * 2 + 1 - core)
    far = (v, lax.rem(sp + 15 + 2 * core, 16))
    vol_peers = [lax.rem(x + i, 4) * 4 + lax.rem(y + j, 4) for i, j in VOL_NEAR_LAST]
    z_peers = [lax.rem(z + i, 8) for i in Z_NEAR_LAST]

    def at_z(k):
        return (v, k * 2 + core)

    def along(places):
        return lax.rem(z + 8 + (1 - 2 * core) * places, 8)

    own_copy = pltpu.make_async_copy(vol, volb.at[1 + core], loc_sem.at[0])
    own_copy.start()
    gw_copy = pltpu.make_async_copy(gw_hbm, gw, loc_sem.at[2])
    gw_copy.start()
    pg_copy = pltpu.make_async_copy(pg_hbm, pg, loc_sem.at[3])
    pg_copy.start()
    w_copy = pltpu.make_async_copy(w, wv, loc_sem.at[1])
    w_copy.start()

    nearest = [
        (lax.rem(x + 1, 4) * 4 + y, sp),
        (lax.rem(x + 3, 4) * 4 + y, sp),
        (x * 4 + lax.rem(y + 1, 4), sp),
        (x * 4 + lax.rem(y + 3, 4), sp),
        at_z(lax.rem(z + 1, 8)),
        at_z(lax.rem(z + 7, 8)),
    ]
    barrier = pltpu.get_barrier_semaphore()
    for device in [sib, far] + nearest:
        pl.semaphore_signal(barrier, inc=1, device_id=device, device_id_type=pl.DeviceIdType.MESH)

    def tell(i):
        for device in nearest:
            pl.semaphore_signal(
                round_sem.at[i], inc=1, device_id=device, device_id_type=pl.DeviceIdType.MESH
            )

    def hear(i):
        pl.semaphore_wait(round_sem.at[i], len(nearest))

    m = iota((384, 256), 0)
    tap, within = lax.div(m, 128), lax.rem(m, 128)
    row = 2 * lax.div(lax.rem(within, 64), 16) + lax.div(within, 64)
    col = 2 * lax.rem(within, 16) + tap - 1
    pick[...] = one_where((iota((384, 256), 1) == row * 32 + col) & (col >= 0))

    pl.semaphore_wait(barrier, 2 + len(nearest))

    def rows_of(chunk):
        return pl.ds(256 * chunk, 256)

    to_far = [
        remote(
            vol.at[rows_of(q)],
            volb.at[3 - 3 * core, rows_of(q)],
            far_send.at[q],
            far_recv.at[q],
            far,
        )
        for q in range(CHUNKS)
    ]
    to_sib = remote(vol, volb.at[1 + core], sib_send.at[0], sib_recv.at[0], sib)
    for copy in to_far:
        copy.start()
    to_sib.start()
    tell(0)

    m, n = iota((256, 256), 0), iota((256, 256), 1)
    in_row = lax.rem(m, 16)
    shift[0] = one_where((n == m - 1) & (in_row != 0))
    shift[1] = one_where((n == m + 1) & (in_row != 15))
    same_group = lax.div(m, 8) == lax.div(n, 8)
    for k in range(3):
        hk[k, 0:16, :] = jnp.zeros((16, 256), BF16)
        hk[k, 272:288, :] = jnp.zeros((16, 256), BF16)
        dk[k, 0:16, :] = jnp.zeros((16, 256), BF16)
        dk[k, 272:288, :] = jnp.zeros((16, 256), BF16)

    def windows(slot, block, inside):
        if block == 0:
            xs[slot, 0:16, 0:384] = jnp.zeros((16, 384), BF16)
        picked = dot(pick[...], volb[slot, 256 * block : 256 * block + 256, :])
        if inside is not None:
            picked = picked * inside
        picked = picked.astype(BF16)
        for e in range(3):
            even = picked[e * 128 : e * 128 + 64]
            odd = picked[e * 128 + 64 : e * 128 + 128]
            for b, rows, offset in ((0, odd, 16), (1, even, 0), (2, odd, 0)):
                lane = (b * 3 + e) * 128
                start = 64 * block + offset
                xs[slot, start : start + 64, lane : lane + 128] = rows

    at_low = jnp.where(z == 0, 0.0, 1.0)
    at_high = jnp.where(z == 7, 0.0, 1.0)
    far_inside = jnp.where(core == 0, at_low, at_high)
    beyond_inside = jnp.where(core == 0, at_high, at_low)

    own_copy.wait()
    for block in range(4):
        windows(1 + core, block, None)
    gw_copy.wait()
    for jk in range(9):
        tiled = jnp.broadcast_to(gw[jk].astype(F32)[None], (32, 8, 256)).reshape(256, 256)
        wg[jk] = jnp.where(same_group, tiled, 0.0).astype(BF16)
    remote(vol, volb.at[2 - core], sib_send.at[0], sib_recv.at[0], sib).wait_recv()
    for block in range(4):
        windows(2 - core, block, None)
    hear(0)
    tell(1)
    w_copy.wait()
    pre = dot(xs[core + 1, 0:256, :], wv[1]) + dot(xs[2 - core, 0:256, :], wv[2 - 2 * core])
    relays = []
    for block in range(4):
        remote(
            vol.at[rows_of(block)],
            volb.at[3 * core, rows_of(block)],
            far_send.at[block],
            far_recv.at[block],
            far,
        ).wait_recv()
        relay = remote(
            volb.at[3 * core, rows_of(block)],
            volb.at[3 * core, rows_of(block)],
            relay_send.at[block],
            relay_recv.at[block],
            sib,
        )
        relay.start()
        relays.append(relay)
        windows(3 * core, block, far_inside)
    pre = pre + dot(xs[3 * core, 0:256, :], wv[2 * core])

    hear(1)
    tell(2)
    pg_copy.wait()
    count = cnt[0]
    live = jnp.where(sp < count, 1.0, 0.0)
    hidden = (jnp.maximum(pre, 0.0) * live).astype(BF16)
    hk[1, 16:272, :] = hidden
    hk[0, 16:272, :] = dot(shift[0], hidden).astype(BF16)
    hk[2, 16:272, :] = dot(shift[1], hidden).astype(BF16)
    summed = hidden.astype(F32)
    for j in range(3):
        for k in range(3):
            summed = summed + dot(hk[k, 16 * j : 16 * j + 256, :], wg[3 * j + k])
    scale = 1.0 / jnp.full((1, 256), count.astype(F32) * 256.0)
    cotangent = pg[...] * live * scale
    d_wide = jnp.where(summed > 0, cotangent, 0.0)
    d_summed = d_wide.astype(BF16)
    dk[1, 16:272, :] = d_summed
    dk[0, 16:272, :] = dot(shift[0], d_summed).astype(BF16)
    dk[2, 16:272, :] = dot(shift[1], d_summed).astype(BF16)
    d_hidden = d_summed.astype(F32)
    for j in range(3):
        for k in range(3):
            lines = dk[2 - k, 16 * (2 - j) : 16 * (2 - j) + 256, :]
            d_hidden = d_hidden + dot_nt(lines, wg[3 * j + k])
    d_pre = jnp.where(pre > 0, d_hidden, 0.0) * live
    turned = d_pre.T.astype(BF16)
    for t in range(8):
        for c in range(2):
            start = 16 * (2 * t + c)
            dts[c, 16 * t : 16 * t + 16, :] = turned[start : start + 16, :]
    swap_d = remote(dts.at[1 - core], dx, dx_send.at[0], dx_recv.at[0], sib)
    swap_d.start()

    for block in range(4):
        remote(
            volb.at[3 - 3 * core, rows_of(block)],
            volb.at[3 - 3 * core, rows_of(block)],
            relay_send.at[block],
            relay_recv.at[block],
            sib,
        ).wait_recv()
        windows(3 - 3 * core, block, beyond_inside)
    swap_d.wait_recv()

    def partial(a, first, end):
        lanes = slice(128 * first, 128 * end)
        total = dot(dts[core], xs[core + a, 0:256, lanes])
        return (total + dot(dx[...], xs[1 - core + a, 0:256, lanes])).astype(BF16)

    place = 0
    for a in range(3):
        first, end = Z_FIRST[a]
        total = partial(a, first, end)
        for q in range(end - first):
            for t in range(8):
                za[t, place + q] = total[16 * t : 16 * t + 16, 128 * q : 128 * q + 128]
        place += end - first
    hear(2)
    z_sends = [
        remote(
            za.at[along(home)], zm.at[i], zm_send.at[i], zm_recv.at[i], at_z(along(stop))
        )
        for i, (home, stop) in enumerate(((4, 2), (3, 1), (-3, -1)))
    ] + [
        remote(za.at[along(o)], zr.at[i], za_send.at[i], za_recv.at[i], at_z(along(o)))
        for i, o in enumerate((1, -1, 2, -2))
    ]
    for copy in z_sends[:3]:
        copy.start()

    place = 0
    for a in range(3):
        first = Z_FIRST[a][0]
        total = partial(a, 0, first)
        for q in range(first):
            for h in range(2):
                va[h, place + q] = total[64 * h : 64 * h + 64, 128 * q : 128 * q + 128]
        place += first
    v_sends = [
        remote(va.at[h, k], vr.at[h, v], va_send.at[h, k], va_recv.at[h, v], (k, sp))
        for h in range(2)
        for k in vol_peers
    ]
    for copy in v_sends:
        copy.start()

    d_turned = d_wide.T.astype(BF16)
    fold = one_where(lax.rem(iota((256, 128), 0), 8) == lax.rem(iota((256, 128), 1), 8))
    lane_tap = lax.div(iota((256, 128), 1), 8)
    grouped = jnp.zeros((256, 128), F32)
    for j in range(3):
        for k in range(3):
            full = dot(d_turned, hk[k, 16 * j : 16 * j + 256, :])
            kept = jnp.where(same_group, full, 0.0).astype(BF16)
            grouped = jnp.where(lane_tap == 3 * j + k, dot(kept, fold), grouped)
    grouped = grouped.astype(BF16)
    for t in range(8):
        for c in range(2):
            start = 16 * (2 * t + c)
            ggs[c, t] = grouped[start : start + 16, :]
    swap_g = remote(ggs.at[1 - core], gx, dx_send.at[1], dx_recv.at[1], sib)
    swap_g.start()
    swap_g.wait_recv()
    ga[...] = (ggs[core].astype(F32) + gx[...].astype(F32)).astype(BF16)
    g_sends = [
        remote(ga.at[k], gr.at[z], ga_send.at[k], ga_recv.at[z], at_z(k)) for k in z_peers
    ]
    for copy in g_sends:
        copy.start()

    for copy in z_sends[3:5]:
        copy.start()
    for copy in z_sends[:3]:
        copy.wait_recv()
    za[along(2)] = (za[along(2)].astype(F32) + zm[0].astype(F32) + zm[1].astype(F32)).astype(BF16)
    za[along(-2)] = (za[along(-2)].astype(F32) + zm[2].astype(F32)).astype(BF16)
    for copy in z_sends[5:]:
        copy.start()

    def over_z(h):
        total = va[h, v].astype(F32)
        for k in reversed(vol_peers):
            remote(
                va.at[0, 0], vr.at[h, k], va_send.at[h, 0], va_recv.at[h, k], (k, sp)
            ).wait_recv()
            total = total + vr[h, k].astype(F32)
        for t in range(4):
            s2[4 * h + t] = total[16 * t : 16 * t + 16, :].astype(BF16)
        for copy, k in zip(s2_sends, z_peers):

            @pl.when(lax.div(k, 4) == h)
            def _(copy=copy):
                copy.start()

    s2_sends = [
        remote(s2.at[k], r2.at[z], s2_send.at[k], s2_recv.at[z], at_z(k)) for k in z_peers
    ]
    over_z(0)

    total = za[z].astype(F32)
    for i in range(4):
        z_sends[3 + i].wait_recv()
        total = total + zr[i].astype(F32)
    b2[0:Z_BLOCKS] = total.astype(BF16)
    total = ga[z].astype(F32)
    for k in reversed(z_peers):
        remote(ga.at[0], gr.at[k], ga_send.at[0], ga_recv.at[k], at_z(k)).wait_recv()
        total = total + gr[k].astype(F32)
    b2[Z_BLOCKS] = total.astype(BF16)
    for k in vol_peers:

        @pl.when(k <= Z_BLOCKS)
        def _(k=k):
            remote(b2.at[k], rb2.at[v], b2_send.at[k], b2_recv.at[v], (k, sp)).start()

    over_z(1)

    total = s2[z].astype(F32)
    for k in reversed(z_peers):
        remote(s2.at[0], r2.at[k], s2_send.at[0], s2_recv.at[k], at_z(k)).wait_recv()
        total = total + r2[k].astype(F32)
    f3[0] = total.astype(BF16)
    outb[v, 0] = total.astype(BF16)

    by_vol = [
        remote(f3.at[0], outb.at[v, 0], f3_send.at[0, k], f3_recv.at[0, v], (k, sp))
        for k in vol_peers
    ]
    by_z = [
        remote(f3.at[1], outb.at[v, 1], f3_send.at[1, k], f3_recv.at[1, v], (k, sp))
        for k in vol_peers
    ]
    for copy in by_vol:
        copy.start()

    @pl.when(v <= Z_BLOCKS)
    def _():
        total = b2[v].astype(F32)
        for k in reversed(vol_peers):
            remote(b2.at[0], rb2.at[k], b2_send.at[0], b2_recv.at[k], (k, sp)).wait_recv()
            total = total + rb2[k].astype(F32)
        f3[1] = total.astype(BF16)
        outb[v, 1] = total.astype(BF16)
        for copy in by_z:
            copy.start()

    for copy in to_far + relays + [to_sib, swap_d, swap_g] + z_sends + v_sends + g_sends + s2_sends:
        copy.wait_send()
    for k in vol_peers:

        @pl.when(k <= Z_BLOCKS)
        def _(k=k):
            remote(b2.at[k], rb2.at[v], b2_send.at[k], b2_recv.at[v], (k, sp)).wait_send()

    for k in reversed(vol_peers):
        remote(
            f3.at[0], outb.at[k, 0], f3_send.at[0, 0], f3_recv.at[0, k], (k, sp)
        ).wait_recv()
    place = 0
    for a in range(3):
        for t in range(Z_FIRST[a][0]):
            conv_out[9 * a + t] = outb[place, 0].astype(F32)
            place += 1
    for copy in by_vol:
        copy.wait_send()

    for k in reversed(vol_peers):

        @pl.when(k <= Z_BLOCKS)
        def _(k=k):
            remote(
                f3.at[1], outb.at[k, 1], f3_send.at[1, 0], f3_recv.at[1, k], (k, sp)
            ).wait_recv()

    place = 0
    for a in range(3):
        for t in range(*Z_FIRST[a]):
            conv_out[9 * a + t] = outb[place, 1].astype(F32)
            place += 1
    last = jnp.concatenate([outb[Z_BLOCKS, 1].astype(F32), jnp.zeros((112, 128), F32)], axis=0)
    group_out[...] = last.T[0:72, 0:16]

    @pl.when(v <= Z_BLOCKS)
    def _():
        for copy in by_z:
            copy.wait_send()


def in_hbm(array):
    return pltpu.with_memory_space_constraint(array, pltpu.HBM)


def local(volume, conv_weight, group_weight, slice_count, pooled_grad):
    vmem = pl.BlockSpec(memory_space=pltpu.VMEM)
    smem = pl.BlockSpec(memory_space=pltpu.SMEM)
    hbm = pl.BlockSpec(memory_space=pltpu.HBM)
    dma = pltpu.SemaphoreType.DMA
    conv, group = pl.pallas_call(
        kernel,
        out_shape=(
            jax.ShapeDtypeStruct((27, 16, 128), F32),
            jax.ShapeDtypeStruct((72, 16), F32),
        ),
        in_specs=[hbm, hbm, hbm, smem, hbm],
        out_specs=(vmem, vmem),
        scratch_shapes=[
            pltpu.VMEM((4, 1024, 128), BF16),
            pltpu.VMEM((3, 1152, 256), BF16),
            pltpu.VMEM((9, 8, 256), BF16),
            pltpu.VMEM((1, 256), F32),
            pltpu.VMEM((4, 272, 1152), BF16),
            pltpu.VMEM((384, 256), BF16),
            pltpu.VMEM((2, 256, 256), BF16),
            pltpu.VMEM((9, 256, 256), BF16),
            pltpu.VMEM((3, 288, 256), BF16),
            pltpu.VMEM((3, 288, 256), BF16),
            pltpu.VMEM((2, 128, 256), BF16),
            pltpu.VMEM((2, 8, 16, 128), BF16),
            pltpu.VMEM((128, 256), BF16),
            pltpu.VMEM((8, 16, 128), BF16),
            pltpu.VMEM((8, Z_BLOCKS, 16, 128), BF16),
            pltpu.VMEM((4, Z_BLOCKS, 16, 128), BF16),
            pltpu.VMEM((3, Z_BLOCKS, 16, 128), BF16),
            pltpu.VMEM((8, 16, 128), BF16),
            pltpu.VMEM((8, 16, 128), BF16),
            pltpu.VMEM((2, 16, 64, 128), BF16),
            pltpu.VMEM((2, 16, 64, 128), BF16),
            pltpu.VMEM((8, 16, 128), BF16),
            pltpu.VMEM((8, 16, 128), BF16),
            pltpu.VMEM((Z_BLOCKS + 1, 16, 128), BF16),
            pltpu.VMEM((16, 16, 128), BF16),
            pltpu.VMEM((2, 16, 128), BF16),
            pltpu.VMEM((16, 2, 16, 128), BF16),
            pltpu.SemaphoreType.REGULAR((3,)),
            dma((4,)),
            dma((1,)),
            dma((1,)),
            dma((CHUNKS,)),
            dma((CHUNKS,)),
            dma((CHUNKS,)),
            dma((CHUNKS,)),
            dma((2,)),
            dma((2,)),
            dma((4,)),
            dma((4,)),
            dma((3,)),
            dma((3,)),
            dma((8,)),
            dma((8,)),
            dma((2, 16)),
            dma((2, 16)),
            dma((8,)),
            dma((8,)),
            dma((16,)),
            dma((16,)),
            dma((2, 16)),
            dma((2, 16)),
        ],
        compiler_params=pltpu.CompilerParams(
            collective_id=0, has_side_effects=True, vmem_limit_bytes=48_000_000
        ),
        cost_estimate=pl.CostEstimate(
            flops=2_500_000_000, bytes_accessed=3_000_000, transcendentals=0
        ),
    )(
        in_hbm(volume.reshape(1024, 128)),
        in_hbm(conv_weight.reshape(3, 1152, 256)),
        in_hbm(group_weight.reshape(9, 8, 256)),
        slice_count,
        in_hbm(pooled_grad),
    )
    conv = conv.reshape(3, 3, 3, 16, 128).swapaxes(3, 4)
    return conv, group.reshape(3, 3, 8, 16)


def solution(mesh):
    in_specs = (P("vol", "sp", None, None, None), P(), P(), P("vol"), P("vol", None))
    out_specs = (P(None, None, None, None, "sp"), P(None, None, None, "sp"))
    return jax.shard_map(local, mesh=mesh, in_specs=in_specs, out_specs=out_specs, check_vma=False)
```
